768 devices in a mesh: curve: 96 (over y, z), sub: 8 (over x, core).
Axes of the slice: x: 4, y: 8, z: 12, core: 2. Of those that a mesh axis runs over, the one named last changes fastest.
Arguments:
- state_now: float32 [5, 125, 98304], P(None, None, ('curve', 'sub')), may hold values from -0.5 to 4, as said below
- section_memory: float32 [5, 125, 98304], P(None, None, ('curve', 'sub')), may hold values from -3 to 3
- element_level: int32 [98304], P(('curve', 'sub')), may hold values from 0 to 1
- face_kind: int32 [6, 98304], P(None, ('curve', 'sub')), may hold values from 0 to 2
- face_partner: int32 [4, 6, 98304], P(None, None, ('curve', 'sub')), may hold values from 0 to 351
- face_quadrant: int32 [6, 98304], P(None, ('curve', 'sub')), may hold values from 0 to 3
- send_sub: int32 [6144, 3, 4], P(('curve', 'sub')), may hold values from 0 to 255
- send_curve: int32 [1536, 3, 32], P(('curve', 'sub')), may hold values from 0 to 255
Outputs:
- state_next: float32 [5, 125, 98304], P(None, None, ('curve', 'sub'))
- memory_next: float32 [5, 125, 98304], P(None, None, ('curve', 'sub'))
The draws below stay inside these ranges and needn't reach their ends.
Inputs may be any that keep to these rules, and one draw needn't show every extreme that they name: `state_now`: density and pressure lie between 0.75 and 1.25 at every point and each velocity component is at most 0.35 in size; the last variable is pressure / 0.4 plus the kinetic energy. `face_partner`: values below 256 name this device's faces of the face's direction (side times 128 plus element); the next 32 the faces received from the sub peers (peer times 4 plus slot); the last 64 those from the previous and then the next curve device. Rows 1 to 3 are read only for faces of kind 2. `send_sub`: each entry names a face of this device of the given direction (side times 128 plus element). `send_curve`: row 0 of a device goes to the previous curve device, row 1 to the next; entries as in send_sub. `face_kind`: 0 conforming, 1 small side of a 2:1 mortar, 2 big side.
All inputs are finite; a program needn't handle non-finite values.
Results may differ from the reference program's by a relative error of at most 0.0003.
Values sent between devices are 32-bit elements; how exact they have to be, the bound alone decides.
No kernel may reach another device: no remote copies, remote signals or barrier semaphores. Data moves between devices by JAX's collectives and lax.ppermute only.
A program may use at most 128 MiB of HBM per device.

```python
import math
import jax
import jax.numpy as jnp
import numpy as np
from jax import lax

VARS = 5
NODES = 125
E_DEV = 128
SX = 4
SC = 32
PD = 352
ELEMS = 98304
N_CURVE = 96
N_SUB = 8
DEVICES = 768


def draw_state_now(key, part):
    key = jax.random.fold_in(key, 11)
    keys = jax.random.split(key, 3)
    density = 1.0 + 0.1 * jax.random.truncated_normal(keys[0], -2.0, 2.0, (NODES, ELEMS), jnp.float32)
    velocity = 0.1 * jax.random.truncated_normal(keys[1], -3.0, 3.0, (3, NODES, ELEMS), jnp.float32)
    pressure = 1.0 + 0.1 * jax.random.truncated_normal(keys[2], -2.0, 2.0, (NODES, ELEMS), jnp.float32)
    momentum = density[None] * velocity
    energy = pressure / 0.4 + 0.5 * density * jnp.sum(velocity * velocity, axis=0)
    return jnp.concatenate([density[None], momentum, energy[None]], axis=0).astype(jnp.float32)


def with_ends(drawn, key, smallest, top_value):
    longest = drawn.shape.index(max(drawn.shape))
    spots = []
    for shift in (0, 1):
        where = [jax.random.randint(jax.random.fold_in(key, axis), (), 0, length) for axis, length in enumerate(drawn.shape)]
        where[longest] = (where[longest] + shift) % drawn.shape[longest]
        spots.append(tuple(where))
    return drawn.at[spots[0]].set(smallest).at[spots[1]].set(top_value)


def block_scale(own_key, dims, pieces, smallest, top_value):
    loudness = 1.0
    for axis_at, shards_of in pieces:
        draws = jax.random.uniform(jax.random.fold_in(jax.random.fold_in(own_key, 6), axis_at), (shards_of,), jnp.float32, smallest / len(pieces), top_value / len(pieces))
        loudness = loudness * jnp.repeat(jnp.exp(draws), dims[axis_at] // shards_of).reshape((-1,) + (1,) * (len(dims) - 1 - axis_at))
    return loudness


def gaussian(stream_key, dims, scale, reach, pieces=(), kind=jnp.bfloat16):
    values = scale * jax.random.normal(stream_key, dims, jnp.float32)
    if pieces:
        values = values * block_scale(stream_key, dims, pieces, -0.22, 0.18)
    return jnp.clip(values, -reach, reach).astype(kind)


def setup_inputs(seed: int = 0) -> dict:
    seeds = jax.random.split(jax.random.key(seed), 9)
    return {
        "state_now": draw_state_now(jax.random.fold_in(seeds[8], 71), 0),
        "section_memory": gaussian(seeds[1], (VARS, NODES, ELEMS), 0.5, 3.0, ((2, 768),), jnp.float32),
        "element_level": with_ends(jax.random.randint(seeds[2], (ELEMS,), 0, 2), jax.random.fold_in(seeds[2], 1), 0, 1).astype(jnp.int32),
        "face_kind": with_ends(jax.random.randint(seeds[3], (6, ELEMS), 0, 3), jax.random.fold_in(seeds[3], 1), 0, 2).astype(jnp.int32),
        "face_partner": with_ends(jax.random.randint(seeds[4], (4, 6, ELEMS), 0, PD), jax.random.fold_in(seeds[4], 1), 0, PD - 1).astype(jnp.int32),
        "face_quadrant": with_ends(jax.random.randint(seeds[5], (6, ELEMS), 0, 4), jax.random.fold_in(seeds[5], 1), 0, 3).astype(jnp.int32),
        "send_sub": with_ends(jax.random.randint(seeds[6], (DEVICES * N_SUB, 3, SX), 0, 2 * E_DEV), jax.random.fold_in(seeds[6], 1), 0, (2 * E_DEV) - 1).astype(jnp.int32),
        "send_curve": with_ends(jax.random.randint(seeds[7], (DEVICES * 2, 3, SC), 0, 2 * E_DEV), jax.random.fold_in(seeds[7], 1), 0, (2 * E_DEV) - 1).astype(jnp.int32),
    }


viscosity = 0.1
conduction = 0.1 * 1.4 / (0.4 * 0.72)
time_step = 0.02
section_decay = -567301805773.0 / 1357537059087.0
section_weight = 5161836677717.0 / 13612068292357.0
highest = lax.Precision.HIGHEST

def gl_tables():
    gl_nodes = np.array([-1.0, -math.sqrt(3.0 / 7.0), 0.0, math.sqrt(3.0 / 7.0), 1.0])
    gl_weights = np.array([0.1, 49.0 / 90.0, 32.0 / 45.0, 49.0 / 90.0, 0.1])
    products = np.array([np.prod([gl_nodes[m] - gl_nodes[k] for k in range(5) if k != m]) for m in range(5)])
    derivative = np.zeros((5, 5))
    for i in range(5):
        for m in range(5):
            if i != m:
                derivative[i, m] = products[i] / products[m] / (gl_nodes[i] - gl_nodes[m])
        derivative[i, i] = -np.sum(derivative[i])

    def lagrange(points):
        values = np.ones((5, 5))
        for m in range(5):
            for k in range(5):
                if k != m:
                    values[:, m] = values[:, m] * (points - gl_nodes[k]) / (gl_nodes[m] - gl_nodes[k])
        return values
    halves = [lagrange((gl_nodes - 1.0) / 2.0), lagrange((gl_nodes + 1.0) / 2.0)]
    projections = [0.5 * (half_map * gl_weights[:, None]).T / gl_weights[:, None] for half_map in halves]
    interp_table = np.stack([np.kron(halves[a], halves[b]) for a in range(2) for b in range(2)])
    project_table = np.stack([np.kron(projections[a], projections[b]) for a in range(2) for b in range(2)])
    return (jnp.asarray(derivative, dtype=jnp.float32), jnp.asarray(interp_table, dtype=jnp.float32), jnp.asarray(project_table, dtype=jnp.float32), float(gl_weights[0]))

def primitives(conserved):
    density = conserved[0]
    velocity = conserved[1:4] / density
    pressure = 0.4 * (conserved[4] - 0.5 * lax.optimization_barrier(jnp.sum(conserved[1:4] * velocity, axis=0)))
    return (density, velocity, pressure)

def euler_flux(conserved, direction):
    density, velocity, pressure = primitives(conserved)
    normal_speed = velocity[direction]
    flux_rows = [conserved[1 + direction]]
    for k in range(3):
        flux_term = conserved[1 + k] * normal_speed
        if k == direction:
            flux_term = flux_term + pressure
        flux_rows.append(flux_term)
    flux_rows.append((conserved[4] + pressure) * normal_speed)
    return jnp.stack(flux_rows)

def signal_speed(conserved, direction):
    density, velocity, pressure = primitives(conserved)
    return jnp.abs(velocity[direction]) + jnp.sqrt(1.4 * pressure / density)

def face_flux(minus_side, plus_side, direction, normal_sign):
    fastest = jnp.maximum(signal_speed(minus_side, direction), signal_speed(plus_side, direction))
    return 0.5 * normal_sign * (euler_flux(minus_side, direction) + euler_flux(plus_side, direction)) - 0.5 * fastest * (plus_side - minus_side)

def gradient_inputs(conserved):
    density, velocity, pressure = primitives(conserved)
    return jnp.concatenate([velocity, (pressure / density)[None]], axis=0)

def viscous_flux(conserved, gradients, direction):
    density, velocity, pressure = primitives(conserved)
    divergence = gradients[0] + gradients[4] + gradients[8]
    stresses = []
    for k in range(3):
        stress = viscosity * (gradients[3 * direction + k] + gradients[3 * k + direction])
        if k == direction:
            stress = stress - 2.0 / 3.0 * viscosity * divergence
        stresses.append(stress)
    heat_flux = velocity[0] * stresses[0] + velocity[1] * stresses[1] + velocity[2] * stresses[2]
    heat_flux = heat_flux + conduction * gradients[9 + direction]
    return jnp.stack(stresses + [heat_flux])

def along_axis(nodal_field, derivative, direction):
    moved_field = jnp.moveaxis(nodal_field, 3 - direction, 3)
    result = jnp.einsum('im,cabmz->cabiz', derivative, moved_field, precision=highest)
    return jnp.moveaxis(result, 3, 3 - direction)

def split_volume(conserved, derivative, direction):
    density, velocity, pressure = primitives(conserved)
    enthalpy = (conserved[4] + pressure) / density

    def paired(nodal_field):
        moved_field = jnp.moveaxis(nodal_field, 2 - direction, 2)
        return 0.5 * (moved_field[:, :, :, None, :] + moved_field[:, :, None, :, :])
    mass_flux = paired(density) * paired(velocity[direction])
    flux_rows = [mass_flux]
    for k in range(3):
        flux_term = mass_flux * paired(velocity[k])
        if k == direction:
            flux_term = flux_term + paired(pressure)
        flux_rows.append(flux_term)
    flux_rows.append(mass_flux * paired(enthalpy))
    volume = 2.0 * jnp.einsum('im,cabimz->cabiz', derivative, jnp.stack(flux_rows), precision=highest)
    return jnp.moveaxis(volume, 3, 3 - direction)

def face_trace(nodal_field, direction, s):
    picked = jnp.take(nodal_field, 4 * s, axis=3 - direction)
    return picked.reshape(picked.shape[0], 25, picked.shape[-1])

def axis_traces(nodal_field, direction):
    return jnp.concatenate([face_trace(nodal_field, direction, 0), face_trace(nodal_field, direction, 1)], axis=-1)

def add_faces(nodal_field, direction, values):
    elements = nodal_field.shape[-1]
    for s in range(2):
        where_face = [slice(None)] * 5
        where_face[3 - direction] = 4 * s
        face_block = values[:, :, s * elements:(s + 1) * elements].reshape(values.shape[0], 5, 5, elements)
        nodal_field = nodal_field.at[tuple(where_face)].add(face_block)
    return nodal_field

def face_signs(elements):
    return jnp.where(jnp.arange(2 * elements) >= elements, 1.0, -1.0).astype(jnp.float32)

def axis_info(face_kind, face_partner, face_quadrant, direction):
    axis_kinds = face_kind[2 * direction:2 * direction + 2].reshape(-1)
    axis_partners = face_partner[:, 2 * direction:2 * direction + 2].reshape(4, -1)
    axis_quadrants = face_quadrant[2 * direction:2 * direction + 2].reshape(-1)
    return (axis_kinds, axis_partners, axis_quadrants)

def mortar_states(pool, own_faces, axis_kinds, axis_partners, axis_quadrants, interp_table):
    first_partner = jnp.take(pool, axis_partners[0], axis=2)
    spread = jnp.einsum('qnm,cmf->qcnf', interp_table, first_partner, precision=highest)
    chosen = axis_quadrants[None, None, None, :] == jnp.arange(4)[:, None, None, None]
    picked = lax.optimization_barrier(jnp.sum(jnp.where(chosen, spread, 0.0), axis=0))
    plus_side = jnp.where(axis_kinds == 1, picked, first_partner)
    minus_parts = jnp.einsum('qnm,cmf->qcnf', interp_table, own_faces, precision=highest)
    plus_parts = jnp.moveaxis(jnp.take(pool, axis_partners, axis=2), 2, 0)
    return (plus_side, minus_parts, plus_parts)

def surface_one(pool, own_faces, axis_kinds, axis_partners, axis_quadrants, direction, normal_sign, tables):
    derivative, interp_table, project_table, edge_weight = tables
    plus_side, minus_parts, plus_parts = mortar_states(pool, own_faces, axis_kinds, axis_partners, axis_quadrants, interp_table)
    is_big = axis_kinds == 2

    def riemann(minus_side, plus_here):
        return face_flux(minus_side, plus_here, direction, normal_sign)

    def average(minus_side, plus_here):
        return 0.5 * (gradient_inputs(minus_side) + gradient_inputs(plus_here))

    def on_mortar(face_rule):
        return jnp.einsum('qmn,qcnf->cmf', project_table, jax.vmap(face_rule)(minus_parts, plus_parts), precision=highest)
    star_flux = jnp.where(is_big, on_mortar(riemann), riemann(own_faces, plus_side))
    inviscid = (star_flux - normal_sign * euler_flux(own_faces, direction)) / edge_weight
    star_vars = jnp.where(is_big, on_mortar(average), average(own_faces, plus_side))
    lifting = normal_sign * (star_vars - gradient_inputs(own_faces)) / edge_weight
    return (inviscid, lifting)

def surface_two(pool_flux, own_flux, axis_kinds, axis_partners, axis_quadrants, normal_sign, tables):
    derivative, interp_table, project_table, edge_weight = tables
    plus_side, minus_parts, plus_parts = mortar_states(pool_flux, own_flux, axis_kinds, axis_partners, axis_quadrants, interp_table)
    mortar_mean = jnp.einsum('qmn,qcnf->cmf', project_table, 0.5 * normal_sign * (minus_parts + plus_parts), precision=highest)
    star_flux = jnp.where(axis_kinds == 2, mortar_mean, 0.5 * normal_sign * (own_flux + plus_side))
    return (star_flux - normal_sign * own_flux) / edge_weight

def local_gradients(conserved, metric, info_list, state_pools, tables):
    derivative = tables[0]
    elements = conserved.shape[-1]
    normal_sign = face_signs(elements)
    lifted_inputs = gradient_inputs(conserved)
    per_direction = []
    inviscid_list = []
    for d in range(3):
        own_faces = axis_traces(conserved, d)
        axis_kinds, axis_partners, axis_quadrants = info_list[d]
        inviscid, lifting = surface_one(state_pools[d], own_faces, axis_kinds, axis_partners, axis_quadrants, d, normal_sign, tables)
        inviscid_list.append(inviscid)
        per_direction.append(add_faces(along_axis(lifted_inputs, derivative, d), d, lifting))
    gradients = jnp.stack(per_direction, axis=1).reshape(12, 5, 5, 5, elements) * metric
    return (gradients, inviscid_list)

def own_viscous(conserved, gradients):
    return [viscous_flux(axis_traces(conserved, d), axis_traces(gradients, d), d) for d in range(3)]

def local_residual(conserved, metric, gradients, inviscid_list, own_fluxes, flux_pools, info_list, tables):
    derivative = tables[0]
    elements = conserved.shape[-1]
    normal_sign = face_signs(elements)
    zero_row = jnp.zeros((1, 5, 5, 5, elements), jnp.float32)
    zero_face = jnp.zeros((1, 25, 2 * elements), jnp.float32)
    residual = jnp.zeros_like(conserved)
    for d in range(3):
        axis_kinds, axis_partners, axis_quadrants = info_list[d]
        viscous_face = surface_two(flux_pools[d], own_fluxes[d], axis_kinds, axis_partners, axis_quadrants, normal_sign, tables)
        viscous_volume = along_axis(viscous_flux(conserved, gradients, d), derivative, d)
        change = jnp.concatenate([zero_row, viscous_volume], axis=0) - split_volume(conserved, derivative, d)
        change = add_faces(change, d, jnp.concatenate([zero_face, viscous_face], axis=0) - inviscid_list[d])
        residual = residual + change
    return residual * metric

def pack_sub(own_lists, send_lists):
    picked = [jnp.take(own_lists[d], send_lists[:, d, :], axis=2) for d in range(3)]
    stacked = jnp.stack(picked, axis=3)
    return stacked.reshape(stacked.shape[0], 25, -1)

def pack_curve(own_lists, send_lists):
    picked = [jnp.take(own_lists[d], send_lists[r, d, :], axis=2) for r in range(2) for d in range(3)]
    return jnp.concatenate(picked, axis=-1)

def assemble_pools(own_lists, arrived, curve_rim, peers, slots_sub, slots_curve):
    components = arrived.shape[0]
    sub_parts = arrived.reshape(components, 25, peers, 3, slots_sub)
    lower_part = curve_rim[:, :, :3 * slots_curve].reshape(components, 25, 3, slots_curve)
    upper_part = curve_rim[:, :, 9 * slots_curve:].reshape(components, 25, 3, slots_curve)
    return [jnp.concatenate([own_lists[d], sub_parts[:, :, :, d, :].reshape(components, 25, peers * slots_sub), lower_part[:, :, d, :], upper_part[:, :, d, :]], axis=-1) for d in range(3)]

def share_reference(own_lists, sub_lists, curve_lists):
    devices = sub_lists.shape[0]
    sub_packs = jax.vmap(pack_sub)(own_lists, sub_lists)
    components = sub_packs.shape[1]
    grouped = sub_packs.reshape(N_CURVE, N_SUB, components, 25, N_SUB, 3 * SX)
    arrived = grouped.transpose(0, 4, 2, 3, 1, 5).reshape(devices, components, 25, N_SUB * 3 * SX)
    curve_packs = jax.vmap(pack_curve)(own_lists, curve_lists).reshape(N_CURVE, N_SUB, components, 25, 6 * SC)
    from_lower = jnp.roll(curve_packs, 1, axis=0)[..., 3 * SC:]
    from_upper = jnp.roll(curve_packs, -1, axis=0)[..., :3 * SC]
    curve_rim = jnp.concatenate([from_lower, curve_packs, from_upper], axis=-1).reshape(devices, components, 25, 12 * SC)

    def assemble_one(own_part, received, rim_part):
        return assemble_pools(own_part, received, rim_part, N_SUB, SX, SC)
    return jax.vmap(assemble_one)(own_lists, arrived, curve_rim)

def reference(state_now, section_memory, element_level, face_kind, face_partner, face_quadrant, send_sub, send_curve):
    tables = gl_tables()
    elements = E_DEV
    devices = N_CURVE * N_SUB
    conserved_all = state_now.reshape(5, 125, devices, elements).transpose(2, 0, 1, 3).reshape(devices, 5, 5, 5, 5, elements)
    metric_all = 1.0 + element_level.reshape(devices, elements).astype(jnp.float32)
    kinds_all = face_kind.reshape(6, devices, elements).transpose(1, 0, 2)
    partners_all = face_partner.reshape(4, 6, devices, elements).transpose(2, 0, 1, 3)
    quadrants_all = face_quadrant.reshape(6, devices, elements).transpose(1, 0, 2)
    sub_lists = send_sub.reshape(devices, N_SUB, 3, SX)
    curve_lists = send_curve.reshape(devices, 2, 3, SC)

    def state_faces(conserved):
        return [axis_traces(conserved, d) for d in range(3)]
    state_pools = share_reference(jax.vmap(state_faces)(conserved_all), sub_lists, curve_lists)

    def gradient_pass(items):
        conserved, metric, kinds, partners, quadrants, pools = items
        info_list = [axis_info(kinds, partners, quadrants, d) for d in range(3)]
        gradients, inviscid_list = local_gradients(conserved, metric, info_list, pools, tables)
        return own_viscous(conserved, gradients)
    flux_traces = lax.map(gradient_pass, (conserved_all, metric_all, kinds_all, partners_all, quadrants_all, state_pools))
    flux_pools = share_reference(flux_traces, sub_lists, curve_lists)

    def residual_pass(items):
        conserved, metric, kinds, partners, quadrants, pools, fluxes = items
        info_list = [axis_info(kinds, partners, quadrants, d) for d in range(3)]
        gradients, inviscid_list = local_gradients(conserved, metric, info_list, pools, tables)
        own_fluxes = own_viscous(conserved, gradients)
        return local_residual(conserved, metric, gradients, inviscid_list, own_fluxes, fluxes, info_list, tables)
    residual = lax.map(residual_pass, (conserved_all, metric_all, kinds_all, partners_all, quadrants_all, state_pools, flux_pools))
    residual = residual.reshape(devices, 5, 125, elements).transpose(1, 2, 0, 3).reshape(5, 125, devices * elements)
    memory_next = section_decay * section_memory + time_step * residual
    state_next = state_now + section_weight * memory_next
    return (state_next, memory_next)
```

```python
import functools
import math

import jax
import jax.numpy as jnp
import ml_dtypes
import numpy as np
from jax import lax
from jax.experimental import pallas as pl
from jax.experimental.pallas import tpu as pltpu
from jax.sharding import PartitionSpec as P

viscosity = 0.1
conduction = 0.1 * 1.4 / (0.4 * 0.72)
time_step = 0.02
section_decay = -567301805773.0 / 1357537059087.0
section_weight = 5161836677717.0 / 13612068292357.0
EDGE = 0.1
F32, BF16 = jnp.float32, jnp.bfloat16
ELEMENTS = 128
VMEM_LIMIT = 56 * 1024 * 1024


def node_tables():
    nodes = np.array([-1.0, -math.sqrt(3.0 / 7.0), 0.0, math.sqrt(3.0 / 7.0), 1.0])
    weights = np.array([0.1, 49.0 / 90.0, 32.0 / 45.0, 49.0 / 90.0, 0.1])
    prods = np.array(
        [np.prod([nodes[m] - nodes[k] for k in range(5) if k != m]) for m in range(5)]
    )
    deriv = np.zeros((5, 5))
    for i in range(5):
        for m in range(5):
            if i != m:
                deriv[i, m] = prods[i] / prods[m] / (nodes[i] - nodes[m])
        deriv[i, i] = -np.sum(deriv[i])

    def lagrange(points):
        values = np.ones((5, 5))
        for m in range(5):
            for k in range(5):
                if k != m:
                    values[:, m] = values[:, m] * (points - nodes[k]) / (nodes[m] - nodes[k])
        return values

    halves = [lagrange((nodes - 1.0) / 2.0), lagrange((nodes + 1.0) / 2.0)]
    projs = [0.5 * (h * weights[:, None]).T / weights[:, None] for h in halves]
    interp = [np.kron(halves[a], halves[b]) for a in range(2) for b in range(2)]
    project = [np.kron(projs[a], projs[b]) for a in range(2) for b in range(2)]
    return deriv, interp, project


def padded(matrix, rows, cols):
    out = np.zeros((rows, cols))
    out[: matrix.shape[0], : matrix.shape[1]] = matrix
    return out


def split_np(matrix):
    high = matrix.astype(np.float32).astype(ml_dtypes.bfloat16)
    low = (matrix - high.astype(np.float64)).astype(np.float32).astype(ml_dtypes.bfloat16)
    return high, low


def stack3(matrix):
    high, low = split_np(matrix)
    return np.concatenate([high, high, low], axis=1)


@functools.lru_cache(maxsize=None)
def constants():
    deriv, interp, project = node_tables()
    eye5 = np.eye(5)
    big = [
        np.kron(np.kron(eye5, eye5), deriv),
        np.kron(np.kron(eye5, deriv), eye5),
        np.kron(np.kron(deriv, eye5), eye5),
    ]
    index = np.arange(125)
    coord = [index % 5, (index // 5) % 5, index // 25]
    trace = {}
    for d in range(3):
        for s in range(2):
            rows = index[coord[d] == 4 * s]
            t = np.zeros((25, 125))
            t[np.arange(25), rows] = 1.0
            trace[d, s] = t
    sigma = (-1.0, 1.0)
    edge_sign = [
        sum(sigma[s] / EDGE * trace[d, s].T @ trace[d, s] for s in range(2)) for d in range(3)
    ]
    out = {}
    out["deriv_all"] = stack3(np.concatenate([padded(big[d], 128, 128) for d in range(3)], axis=0))
    out["deriv_sum"] = np.concatenate([stack3(padded(big[d], 128, 128)) for d in range(3)], axis=1)
    out["own"] = np.stack(
        [
            np.concatenate(
                [
                    stack3(padded(m @ trace[d, s], 32, 128))
                    for s in range(2)
                    for m in [np.eye(25)] + interp
                ],
                axis=0,
            )
            for d in range(3)
        ]
    )
    spread = np.zeros((160, 128))
    for c in range(5):
        spread[c * 32 : c * 32 + 25, c * 25 : c * 25 + 25] = np.eye(25)
    out["spread"] = spread.astype(ml_dtypes.bfloat16)
    out["quads"] = stack3(np.concatenate([padded(interp[q], 32, 32) for q in range(4)], axis=0))
    out["lift"] = np.stack(
        [
            stack3(
                np.concatenate(
                    [
                        padded(0.5 / EDGE * trace[d, s].T @ m, 128, 32)
                        for s in range(2)
                        for m in project + [np.eye(25)]
                    ],
                    axis=1,
                )
            )
            for d in range(3)
        ]
    )

    def packer(comps, d):
        m = np.zeros((256, comps * 128))
        for s in range(2):
            for c in range(comps):
                m[s * 128 + c * 25 : s * 128 + c * 25 + 25, c * 128 : c * 128 + 125] = trace[d, s]
        return m.astype(ml_dtypes.bfloat16)

    out["pack_state"] = np.stack([packer(5, d) for d in range(3)])
    out["pack_flux"] = np.stack([packer(4, d) for d in range(3)])
    both = sum(project[q] @ interp[q] for q in range(4))
    own_visc = []
    for d in range(3):
        own_visc.append(stack3(padded(big[d] - 0.5 * edge_sign[d], 128, 128)))
        own_visc.append(
            stack3(
                padded(
                    sum(
                        0.5 * sigma[s] / EDGE * trace[d, s].T @ (both - np.eye(25)) @ trace[d, s]
                        for s in range(2)
                    ),
                    128,
                    128,
                )
            )
        )
    out["own_visc"] = np.concatenate(own_visc, axis=1)
    out["face_rows"] = np.stack(
        [
            np.concatenate([padded(trace[d, s], 32, 128) for s in range(2)], axis=0)
            for d in range(3)
        ]
    ).astype(ml_dtypes.bfloat16)
    out["visc"] = np.stack(
        [
            stack3(
                np.concatenate(
                    [
                        padded(0.5 * sigma[s] / EDGE * trace[d, s].T @ m, 128, 32)
                        for s in range(2)
                        for m in [np.eye(25)] + interp + project
                    ],
                    axis=1,
                )
            )
            for d in range(3)
        ]
    )
    signs = np.zeros((3, 128, 128), np.float32)
    for d in range(3):
        signs[d, :125, :] = np.diag(edge_sign[d])[:, None]
    out["signs"] = signs
    return out


def split(x):
    high = x.astype(BF16)
    return high, (x - high.astype(F32)).astype(BF16)


def dot(a, b):
    return lax.dot_general(a, b, (((1,), (0,)), ((), ())), preferred_element_type=F32)


def dot_nt(a, b):
    return lax.dot_general(a, b, (((1,), (1,)), ((), ())), preferred_element_type=F32)


def lanes(parts):
    return jnp.concatenate(parts, axis=1)


def rows(parts):
    return jnp.concatenate(parts, axis=0)


def one_hot(index_row, count):
    width = index_row.shape[1]
    numbers = lax.broadcasted_iota(jnp.int32, (count, width), 0)
    return jnp.where(numbers == index_row, 1.0, 0.0).astype(BF16)


def load_padded(ref, pad, count):
    for c in range(count):
        pad[c, 120:128, :] = jnp.full((8, ELEMENTS), 1.0 if c in (0, 4) else 0.0, F32)
        pad[c, 0:125, :] = ref[c]


def point_values(u):
    inverse = 1.0 / u[0]
    vel = [u[1 + k] * inverse for k in range(3)]
    kinetic = u[1] * vel[0] + u[2] * vel[1] + u[3] * vel[2]
    pressure = 0.4 * (u[4] - 0.5 * kinetic)
    return inverse, vel, pressure


def send_pack(high, low, pick_ref, outs):
    data = rows([lanes(high), lanes(low)])
    for t in range(3):
        hot = rows([one_hot(pick_ref[t, d : d + 1, :], 256) for d in range(3)])
        both = dot(data, hot)
        block = both[0:128] + both[128:256]
        outs[t][...] = jnp.transpose(block)[0 : outs[t].shape[0]]


def pack_kernel(state_ref, pick_ref, pack_ref, sub_ref, first_ref, second_ref, pad):
    load_padded(state_ref, pad, 5)
    parts = [split(pad[c]) for c in range(5)]
    right = rows([lanes([h, l]) for h, l in parts])
    high, low = [], []
    for d in range(3):
        both = dot(pack_ref[d], right).astype(BF16)
        high.append(lanes([both[0:128, 0:128], both[128:256, 0:128]]))
        low.append(lanes([both[0:128, 128:256], both[128:256, 128:256]]))
    send_pack(high, low, pick_ref, (sub_ref, first_ref, second_ref))


def volume_kernel(state_ref, all_ref, sum_ref, sign_ref, vol_ref, grad_ref, pad, res):
    load_padded(state_ref, pad, 5)
    u = [pad[c] for c in range(5)]
    inverse, vel, pressure = point_values(u)
    total = u[4] + pressure
    enthalpy = total * inverse
    temperature = pressure * inverse
    fields = [u[0], vel[0], vel[1], vel[2], u[1], u[2], u[3], enthalpy, total, temperature]
    for f, value in enumerate(fields):
        h, l = split(value)
        res[:, f * 128 : (f + 1) * 128] = dot(all_ref[...], rows([h, l, h]))

    def der(f, d):
        return res[d * 128 : (d + 1) * 128, f * 128 : (f + 1) * 128]

    for d in range(3):
        for v, f in enumerate((1, 2, 3, 9)):
            grad_ref[3 * v + d] = der(f, d) - sign_ref[d] * fields[f]
    div_vel = der(1, 0) + der(2, 1) + der(3, 2)
    div_mom = der(4, 0) + der(5, 1) + der(6, 2)
    advect = vel[0] * der(0, 0) + vel[1] * der(0, 1) + vel[2] * der(0, 2)
    carry = advect + div_mom
    mass = 0.5 * (u[0] * div_vel + carry)
    edge_mass = sign_ref[0] * u[1] + sign_ref[1] * u[2] + sign_ref[2] * u[3]
    vol_ref[0] = edge_mass - mass
    specific = [vel[0], vel[1], vel[2], enthalpy]
    full = [u[1], u[2], u[3], total]
    for k in range(4):
        cross = []
        direct = []
        edge = None
        for d in range(3):
            product = full[k] * vel[d]
            flux = product + pressure if k == d else product
            edge_d = sign_ref[d] * flux
            edge = edge_d if edge is None else edge + edge_d
            h, l = split(specific[k] * vel[d])
            cross += [h, l, h]
            h, l = split(product + 4.0 * pressure if k == d else product)
            direct += [h, l, h]
        both = dot(sum_ref[...], lanes([rows(cross), rows(direct)]))
        f_spec, f_full = (1 + k, 4 + k) if k < 3 else (7, 8)
        quad = full[k] * div_vel + specific[k] * carry + u[0] * both[:, 0:128] + both[:, 128:256]
        for d in range(3):
            quad = quad + u[1 + d] * der(f_spec, d) + vel[d] * der(f_full, d)
        vol_ref[1 + k] = edge - 0.25 * quad


def partner_rows(index, d):
    peer = 256 + lax.shift_right_logical(index - 256, 2) * 16 + (index & 3) + 4 * d
    return jnp.where(index < 256, index, jnp.where(index < 288, peer, index + 96))


def gather_hot(partner_ref, kind_ref, parity, d):
    blocks = []
    for q in range(4):
        for s in range(2):
            f = 2 * d + s
            index = partner_ref[q, f : f + 1, :]
            index = jnp.where(index >= 288, swap_curve(index, parity), index)
            row = partner_rows(index, d)
            if q > 0:
                row = jnp.where(kind_ref[f : f + 1, :] == 2, row, -1)
            blocks.append(one_hot(row, 448))
    return lanes(blocks)


def swap_curve(index, parity):
    other = jnp.where(index < 320, index + 32, index - 32)
    return jnp.where(parity == 0, other, index)


def remote_pool(sub_ref, first_ref, second_ref, spread, d):
    arrived = rows(
        [sub_ref[...], first_ref[32 * d : 32 * d + 32, :], second_ref[32 * d : 32 * d + 32, :]]
    )
    h, l = split(arrived)
    return dot_nt(spread, h).astype(BF16), dot_nt(spread, l).astype(BF16)


def surface_kernel(
    parity_ref,
    state_ref,
    grad_in_ref,
    vol_ref,
    level_ref,
    kind_ref,
    partner_ref,
    quadrant_ref,
    sub_ref,
    first_ref,
    second_ref,
    pick_ref,
    own_ref,
    spread_ref,
    quads_ref,
    lift_ref,
    pack_ref,
    acc_ref,
    flux_ref,
    sub_out,
    first_out,
    second_out,
    pad,
    own,
    got,
    quad,
    grad,
):
    parity = parity_ref[0]
    load_padded(state_ref, pad, 5)
    parts = [split(pad[c]) for c in range(5)]
    high = lanes([h for h, l in parts])
    low = lanes([l for h, l in parts])
    right = rows([high, low, high])
    metric = 1.0 + level_ref[...].astype(F32)
    spare = jnp.where(
        lax.broadcasted_iota(jnp.int32, (32, ELEMENTS), 0) >= 25, 1.0, 0.0
    ).astype(F32)
    acc = [vol_ref[c] for c in range(5)]
    for c in range(5):
        acc_ref[c] = vol_ref[c]
    for d in range(3):
        own[...] = dot(own_ref[d], right)
        pool_h, pool_l = [], []
        for s in range(2):
            h, l = split(own[s * 160 : s * 160 + 32, :])
            pool_h.append(rows([h[:, c * 128 : (c + 1) * 128] for c in range(5)]))
            pool_l.append(rows([l[:, c * 128 : (c + 1) * 128] for c in range(5)]))
        far_h, far_l = remote_pool(sub_ref, first_ref, second_ref, spread_ref[...], d)
        pool = rows([lanes(pool_h + [far_h]), lanes(pool_l + [far_l])])
        hot = gather_hot(partner_ref, kind_ref, parity, d)
        both = dot(pool, hot)
        got[...] = both[0:160] + both[160:320]
        parts = [split(got[c * 32 : (c + 1) * 32, 0:256]) for c in range(5)]
        first_h = lanes([h for h, l in parts])
        first_l = lanes([l for h, l in parts])
        quad[...] = dot(quads_ref[...], rows([first_h, first_l, first_h]))
        stacks = {}
        for s in range(2):
            f = 2 * d + s
            sign = 2 * s - 1
            kind = jnp.broadcast_to(kind_ref[f : f + 1, :], (32, ELEMENTS))
            quarter = jnp.broadcast_to(quadrant_ref[f : f + 1, :], (32, ELEMENTS))
            is_big = kind == 2
            is_small = kind == 1
            for q in range(4):
                left, far = [], []
                for c in range(5):
                    spot = slice(c * 128, (c + 1) * 128)
                    minus = own[s * 160 + 32 * (q + 1) : s * 160 + 32 * (q + 2), spot]
                    plus = got[
                        c * 32 : (c + 1) * 32, q * 256 + s * 128 : q * 256 + (s + 1) * 128
                    ]
                    if q == 0:
                        minus = jnp.where(is_big, minus, own[s * 160 : s * 160 + 32, spot])
                        wide = slice(c * 256 + s * 128, c * 256 + (s + 1) * 128)
                        part = quad[96:128, wide]
                        for t in (2, 1, 0):
                            part = jnp.where(quarter == t, quad[32 * t : 32 * t + 32, wide], part)
                        plus = jnp.where(is_small, part, plus)
                    if c in (0, 4):
                        minus = minus + spare
                        plus = plus + spare
                    left.append(minus)
                    far.append(plus)
                if q > 0:
                    far[0] = jnp.where(is_big, far[0], 1.0)
                inv_l, vel_l, press_l = point_values(left)
                inv_r, vel_r, press_r = point_values(far)
                temp_l, temp_r = press_l * inv_l, press_r * inv_r
                speed = jnp.maximum(
                    jnp.abs(vel_l[d]) + jnp.sqrt(1.4 * temp_l),
                    jnp.abs(vel_r[d]) + jnp.sqrt(1.4 * temp_r),
                )
                values = []
                for c in range(5):
                    if c == 0:
                        central = left[1 + d] + far[1 + d]
                    elif c == 4:
                        central = (left[4] + press_l) * vel_l[d] + (far[4] + press_r) * vel_r[d]
                    else:
                        central = left[c] * vel_l[d] + far[c] * vel_r[d]
                        if c == 1 + d:
                            central = central + (press_l + press_r)
                    jump = speed * (far[c] - left[c])
                    values.append(jump - central if sign > 0 else jump + central)
                for a, b in zip(vel_l + [temp_l], vel_r + [temp_r]):
                    values.append(a + b if sign > 0 else -a - b)
                picked = [split(jnp.where(is_big, v, 0.0)) for v in values]
                stacks[s, q] = [lanes([p[j] for p in picked]) for j in range(2)]
                if q == 0:
                    plain = [split(jnp.where(is_big, 0.0, v)) for v in values]
                    stacks[s, 4] = [lanes([p[j] for p in plain]) for j in range(2)]
        stack_h = rows([stacks[s, b][0] for s in range(2) for b in range(5)])
        stack_l = rows([stacks[s, b][1] for s in range(2) for b in range(5)])
        lifted = dot(lift_ref[d], rows([stack_h, stack_l, stack_h]))
        for c in range(5):
            acc_ref[c] = acc_ref[c] + lifted[:, c * 128 : (c + 1) * 128]
        for v in range(4):
            grad[3 * v + d] = metric * (
                grad_in_ref[3 * v + d] + lifted[:, (5 + v) * 128 : (6 + v) * 128]
            )
    inverse = 1.0 / pad[0]
    vel = [pad[1 + k] * inverse for k in range(3)]
    divergence = (2.0 / 3.0 * viscosity) * (grad[0] + grad[4] + grad[8])
    for d in range(3):
        heat = conduction * grad[9 + d]
        for k in range(3):
            tau = viscosity * (grad[3 * d + k] + grad[3 * k + d])
            if k == d:
                tau = tau - divergence
            flux_ref[d, k] = tau
            heat = heat + vel[k] * tau
        flux_ref[d, 3] = heat
    high, low = [], []
    for d in range(3):
        right = rows([lanes(list(split(flux_ref[d, c]))) for c in range(4)])
        both = dot(pack_ref[d], right).astype(BF16)
        high.append(lanes([both[0:128, 0:128], both[128:256, 0:128]]))
        low.append(lanes([both[0:128, 128:256], both[128:256, 128:256]]))
    send_pack(high, low, pick_ref, (sub_out, first_out, second_out))


def own_viscous_kernel(flux_ref, acc_in_ref, kind_ref, matrix_ref, acc_ref):
    numbers = lax.broadcasted_iota(jnp.int32, (128, ELEMENTS), 0)
    places = (numbers % 5, (numbers // 5) % 5, numbers // 25)
    parts = []
    for d in range(3):
        at = places[d]
        low_big = jnp.broadcast_to(kind_ref[2 * d : 2 * d + 1, :], (128, ELEMENTS)) == 2
        high_big = jnp.broadcast_to(kind_ref[2 * d + 1 : 2 * d + 2, :], (128, ELEMENTS)) == 2
        big = ((at == 0) & low_big) | ((at == 4) & high_big)
        plain = [split(flux_ref[d, c]) for c in range(4)]
        masked = [split(jnp.where(big, flux_ref[d, c], 0.0)) for c in range(4)]
        for group in (plain, masked):
            h = lanes([p[0] for p in group])
            l = lanes([p[1] for p in group])
            parts += [h, l, h]
    both = dot(matrix_ref[...], rows(parts))
    acc_ref[0] = acc_in_ref[0]
    for c in range(4):
        acc_ref[1 + c] = acc_in_ref[1 + c] + both[:, c * 128 : (c + 1) * 128]


def final_kernel(
    parity_ref,
    state_ref,
    memory_ref,
    level_ref,
    kind_ref,
    partner_ref,
    quadrant_ref,
    flux_ref,
    acc_in_ref,
    sub_ref,
    first_ref,
    second_ref,
    faces_ref,
    spread_ref,
    visc_ref,
    state_out,
    memory_out,
    acc,
):
    parity = parity_ref[0]
    for d in range(3):
        parts = [split(flux_ref[d, c]) for c in range(4)]
        traces = dot(
            faces_ref[d], lanes([p[0] for p in parts] + [p[1] for p in parts])
        ).astype(BF16)
        pool = []
        far = remote_pool(sub_ref, first_ref, second_ref, spread_ref[0:128], d)
        for j in range(2):
            near = [
                rows(
                    [
                        traces[s * 32 : (s + 1) * 32, (4 * j + c) * 128 : (4 * j + c + 1) * 128]
                        for c in range(4)
                    ]
                )
                for s in range(2)
            ]
            pool.append(lanes(near + [far[j]]))
        hot = gather_hot(partner_ref, kind_ref, parity, d)
        got = dot(rows(pool), hot).astype(BF16)
        stacks = [[], []]
        for s in range(2):
            f = 2 * d + s
            kind = jnp.broadcast_to(kind_ref[f : f + 1, :], (32, ELEMENTS))
            quarter = jnp.broadcast_to(quadrant_ref[f : f + 1, :], (32, ELEMENTS))
            group = jnp.where(kind == 1, quarter + 1, jnp.where(kind == 2, 5, 0))
            wanted = [
                jnp.where(group == t, 1.0, 0.0).astype(BF16) for t in range(6)
            ]
            for j in range(2):
                for b in range(9):
                    q = max(0, b - 5)
                    spot = slice(q * 256 + s * 128, q * 256 + (s + 1) * 128)
                    pieces = [
                        got[j * 128 + c * 32 : j * 128 + (c + 1) * 32, spot] for c in range(4)
                    ]
                    if b < 6:
                        pieces = [p * wanted[b] for p in pieces]
                    stacks[j].append(lanes(pieces))
        high = rows(stacks[0])
        low = rows(stacks[1])
        lifted = dot(visc_ref[d], rows([high, low, high]))
        for c in range(4):
            piece = lifted[:, c * 128 : (c + 1) * 128]
            before = acc_in_ref[1 + c] if d == 0 else acc[c]
            acc[c] = before + piece
    metric = time_step * (1.0 + level_ref[...].astype(F32))
    for c in range(5):
        total = acc_in_ref[0] if c == 0 else acc[c - 1]
        change = section_decay * memory_ref[c] + metric * total[0:125]
        memory_out[c] = change
        state_out[c] = state_ref[c] + section_weight * change


def call(body, outs, operands, scratch=(), scalars=0, cost=None):
    specs = [pl.BlockSpec(memory_space=pltpu.SMEM)] * scalars + [
        pl.BlockSpec(memory_space=pltpu.VMEM)
    ] * (len(operands) - scalars)
    return pl.pallas_call(
        body,
        out_shape=[jax.ShapeDtypeStruct(shape, F32) for shape in outs],
        in_specs=specs,
        out_specs=[pl.BlockSpec(memory_space=pltpu.VMEM)] * len(outs),
        scratch_shapes=[pltpu.VMEM(shape, F32) for shape in scratch],
        compiler_params=pltpu.CompilerParams(vmem_limit_bytes=VMEM_LIMIT),
        name=body.__name__,
        interpret=INTERPRET,
    )(*operands)


INTERPRET = False


def exchange(sub, first, second):
    count = lax.axis_size("curve")
    even_up = [(i, i ^ 1) for i in range(count)]
    odd_up = [(i, (i + 1) % count if i % 2 else (i - 1) % count) for i in range(count)]
    return (
        lax.all_to_all(sub, "sub", split_axis=0, concat_axis=0, tiled=True),
        lax.ppermute(first, "curve", even_up),
        lax.ppermute(second, "curve", odd_up),
    )


def picks(send_sub, send_curve, parity):
    place = np.arange(128)
    sub_rows = jnp.pad(send_sub.reshape(8, 12), ((0, 0), (0, 4))).reshape(1, 128)
    curve_rows = jnp.pad(send_curve.reshape(2, 96), ((0, 0), (0, 32)))
    first = jnp.where(parity == 0, curve_rows[1:2], curve_rows[0:1])
    second = jnp.where(parity == 0, curve_rows[0:1], curve_rows[1:2])
    table = jnp.stack([sub_rows, first, second])
    direction = np.stack([(place % 16) // 4, place // 32, place // 32])
    mask = direction[:, None, :] == np.arange(3)[None, :, None]
    return jnp.where(mask, table, -1)


def local(
    state_now,
    section_memory,
    element_level,
    face_kind,
    face_partner,
    face_quadrant,
    send_sub,
    send_curve,
):
    const = {name: jnp.asarray(value) for name, value in constants().items()}
    parity = (lax.axis_index("curve") % 2).astype(jnp.int32)
    parity_arg = parity.reshape(1)
    level = element_level.reshape(1, ELEMENTS)
    pick = picks(send_sub, send_curve, parity)
    messages = [(128, 128), (96, 128), (96, 128)]
    padded5 = (5, 128, ELEMENTS)
    sent = call(
        pack_kernel, messages, (state_now, pick, const["pack_state"]), scratch=[padded5]
    )
    arrived = exchange(*sent)
    volume, gradients = call(
        volume_kernel,
        [padded5, (12, 128, ELEMENTS)],
        (state_now, const["deriv_all"], const["deriv_sum"], const["signs"]),
        scratch=[padded5, (384, 1280)],
    )
    acc, flux, *sent = call(
        surface_kernel,
        [padded5, (3, 4, 128, ELEMENTS)] + messages,
        (
            parity_arg,
            state_now,
            gradients,
            volume,
            level,
            face_kind,
            face_partner,
            face_quadrant,
            *arrived,
            pick,
            const["own"],
            const["spread"],
            const["quads"],
            const["lift"],
            const["pack_flux"],
        ),
        scratch=[padded5, (320, 640), (160, 1024), (128, 1280), (12, 128, ELEMENTS)],
        scalars=1,
    )
    arrived = exchange(*sent)
    (acc,) = call(
        own_viscous_kernel, [padded5], (flux, acc, face_kind, const["own_visc"])
    )
    state_next, memory_next = call(
        final_kernel,
        [(5, 125, ELEMENTS)] * 2,
        (
            parity_arg,
            state_now,
            section_memory,
            level,
            face_kind,
            face_partner,
            face_quadrant,
            flux,
            acc,
            *arrived,
            const["face_rows"],
            const["spread"],
            const["visc"],
        ),
        scratch=[(4, 128, ELEMENTS)],
        scalars=1,
    )
    return (state_next, memory_next)


def solution(mesh):
    placed = (
        P(None, None, ("curve", "sub")),
        P(None, None, ("curve", "sub")),
        P(("curve", "sub")),
        P(None, ("curve", "sub")),
        P(None, None, ("curve", "sub")),
        P(None, ("curve", "sub")),
        P(("curve", "sub"), None, None),
        P(("curve", "sub"), None, None),
    )
    return jax.shard_map(
        local,
        mesh=mesh,
        in_specs=placed,
        out_specs=(P(None, None, ("curve", "sub")), P(None, None, ("curve", "sub"))),
        check_vma=False,
    )
```

```python
import functools
import math

import jax
import jax.numpy as jnp
import ml_dtypes
import numpy as np
from jax import lax
from jax.experimental import pallas as pl
from jax.experimental.pallas import tpu as pltpu
from jax.sharding import PartitionSpec as P

viscosity = 0.1
conduction = 0.1 * 1.4 / (0.4 * 0.72)
time_step = 0.02
section_decay = -567301805773.0 / 1357537059087.0
section_weight = 5161836677717.0 / 13612068292357.0
EDGE = 0.1
F32, BF16 = jnp.float32, jnp.bfloat16
ELEMENTS = 128
VMEM_LIMIT = 56 * 1024 * 1024


def node_tables():
    nodes = np.array([-1.0, -math.sqrt(3.0 / 7.0), 0.0, math.sqrt(3.0 / 7.0), 1.0])
    weights = np.array([0.1, 49.0 / 90.0, 32.0 / 45.0, 49.0 / 90.0, 0.1])
    prods = np.array(
        [np.prod([nodes[m] - nodes[k] for k in range(5) if k != m]) for m in range(5)]
    )
    deriv = np.zeros((5, 5))
    for i in range(5):
        for m in range(5):
            if i != m:
                deriv[i, m] = prods[i] / prods[m] / (nodes[i] - nodes[m])
        deriv[i, i] = -np.sum(deriv[i])

    def lagrange(points):
        values = np.ones((5, 5))
        for m in range(5):
            for k in range(5):
                if k != m:
                    values[:, m] = values[:, m] * (points - nodes[k]) / (nodes[m] - nodes[k])
        return values

    halves = [lagrange((nodes - 1.0) / 2.0), lagrange((nodes + 1.0) / 2.0)]
    projs = [0.5 * (h * weights[:, None]).T / weights[:, None] for h in halves]
    interp = [np.kron(halves[a], halves[b]) for a in range(2) for b in range(2)]
    project = [np.kron(projs[a], projs[b]) for a in range(2) for b in range(2)]
    return deriv, interp, project


def padded(matrix, rows, cols):
    out = np.zeros((rows, cols))
    out[: matrix.shape[0], : matrix.shape[1]] = matrix
    return out


def split_np(matrix):
    high = matrix.astype(np.float32).astype(ml_dtypes.bfloat16)
    low = (matrix - high.astype(np.float64)).astype(np.float32).astype(ml_dtypes.bfloat16)
    return high, low


def stack3(matrix):
    high, low = split_np(matrix)
    return np.concatenate([high, high, low], axis=1)


def stack2(matrix):
    high, low = split_np(matrix)
    top = np.concatenate([high, high], axis=1)
    return np.concatenate([top, np.concatenate([low, np.zeros_like(low)], axis=1)], axis=0)


@functools.lru_cache(maxsize=None)
def constants():
    deriv, interp, project = node_tables()
    eye5 = np.eye(5)
    big = [
        np.kron(np.kron(eye5, eye5), deriv),
        np.kron(np.kron(eye5, deriv), eye5),
        np.kron(np.kron(deriv, eye5), eye5),
    ]
    index = np.arange(125)
    coord = [index % 5, (index // 5) % 5, index // 25]
    trace = {}
    for d in range(3):
        for s in range(2):
            rows = index[coord[d] == 4 * s]
            t = np.zeros((25, 125))
            t[np.arange(25), rows] = 1.0
            trace[d, s] = t
    sigma = (-1.0, 1.0)
    out = {}
    out["deriv"] = np.stack(
        [np.concatenate(split_np(padded(big[d], 128, 128)), axis=1) for d in range(3)]
    )
    spread = np.zeros((160, 128))
    for c in range(5):
        spread[c * 32 : c * 32 + 25, c * 25 : c * 25 + 25] = np.eye(25)
    out["spread"] = spread.astype(ml_dtypes.bfloat16)
    for comps, name in ((5, "compact_state"), (4, "compact_flux")):
        out[name] = np.tile(spread[: 32 * comps].T, (1, 2)).astype(ml_dtypes.bfloat16)
    out["quads"] = stack3(np.concatenate([padded(interp[q], 32, 32) for q in range(4)], axis=0))
    out["project"] = stack2(np.concatenate([padded(project[q], 32, 32) for q in range(4)], axis=1))
    both = sum(project[q] @ interp[q] for q in range(4))
    mixers = [np.eye(25)] + interp + project + [both - np.eye(25)]
    out["mixers"] = stack2(np.concatenate([padded(m, 32, 32) for m in mixers], axis=1))
    out["faces"] = np.stack(
        [
            np.concatenate([padded(trace[d, s], 32, 128) for s in range(2)], axis=0)
            for d in range(3)
        ]
    ).astype(ml_dtypes.bfloat16)
    for name, signed in (("place_state", False), ("place_flux", True)):
        out[name] = np.stack(
            [
                np.concatenate(
                    [
                        padded((sigma[s] if signed else 1.0) * 5.0 * trace[d, s].T, 128, 32)
                        for s in (0, 1, 0, 1)
                    ],
                    axis=1,
                )
                for d in range(3)
            ]
        ).astype(ml_dtypes.bfloat16)
    return out


def split(x):
    high = x.astype(BF16)
    return high, (x - high.astype(F32)).astype(BF16)


def dot(a, b):
    return lax.dot_general(a, b, (((1,), (0,)), ((), ())), preferred_element_type=F32)


def dot_two(a, high, low):
    both = dot(a, rows([high, low]))
    half = a.shape[0] // 2
    return both[0:half] + both[half:]


def dot_nt(a, b):
    return lax.dot_general(a, b, (((1,), (1,)), ((), ())), preferred_element_type=F32)


def lanes(parts):
    return jnp.concatenate(parts, axis=1)


def rows(parts):
    return jnp.concatenate(parts, axis=0)


def one_hot(index_row, count):
    width = index_row.shape[1]
    numbers = lax.broadcasted_iota(jnp.int32, (count, width), 0)
    return jnp.where(numbers == index_row, 1.0, 0.0).astype(BF16)


def load_padded(ref, pad, count):
    for c in range(count):
        pad[c, 120:128, :] = jnp.full((8, ELEMENTS), 1.0 if c in (0, 4) else 0.0, F32)
        pad[c, 0:125, :] = ref[c]


def point_values(u):
    inverse = 1.0 / u[0]
    vel = [u[1 + k] * inverse for k in range(3)]
    kinetic = u[1] * vel[0] + u[2] * vel[1] + u[3] * vel[2]
    pressure = 0.4 * (u[4] - 0.5 * kinetic)
    return inverse, vel, pressure


def sent_faces(sub_ref, curve_ref):
    place = lax.broadcasted_iota(jnp.int32, (1, 128), 1)
    spot = lax.broadcasted_iota(jnp.int32, (4, 128), 0)
    peer = lax.broadcasted_iota(jnp.int32, (8, 128), 1)
    peers = jnp.where(
        lax.shift_right_logical(peer, 4) == lax.broadcasted_iota(jnp.int32, (8, 128), 0), 1.0, 0.0
    ).astype(BF16)
    slot = lax.broadcasted_iota(jnp.int32, (32, 128), 1)
    slots = jnp.where(
        (slot & 31) == lax.broadcasted_iota(jnp.int32, (32, 128), 0), 1.0, 0.0
    ).astype(BF16)
    sub, lower, upper = [], [], []
    for d in range(3):
        wide = dot(sub_ref[d].astype(F32).astype(BF16), peers)
        wide = jnp.where((place & 3) == spot, wide, 0.0)
        row = jnp.sum(wide, axis=0, keepdims=True).astype(jnp.int32)
        sub.append(jnp.where((lax.shift_right_logical(place, 2) & 3) == d, row, -1))
        wide = dot(curve_ref[d].astype(F32).astype(BF16), slots).astype(jnp.int32)
        here = lax.shift_right_logical(place, 5) == d
        lower.append(jnp.where(here, wide[1:2], -1))
        upper.append(jnp.where(here, wide[0:1], -1))
    return sub, lower, upper


def face_values(faces, parts):
    return dot(faces, lanes([p[0] for p in parts] + [p[1] for p in parts])).astype(BF16)


def pool_rows(traces, count):
    def block(j, c):
        spot = slice((j * count + c) * 128, (j * count + c + 1) * 128)
        return lanes([traces[0:32, spot], traces[32:64, spot]])

    return [rows([block(j, c) for c in range(count)]) for j in range(2)]


def send_pack(traces, count, picks, compact, outs):
    data = lanes([rows(pool_rows(traces[d], count)) for d in range(3)])
    hot = lanes(
        [rows([one_hot(picks[t][d], 256) for d in range(3)]) for t in range(3)]
    )
    found = dot(compact, dot(data, hot).astype(BF16))
    for t in range(3):
        outs[t][...] = jnp.transpose(found[:, t * 128 : (t + 1) * 128])[0 : outs[t].shape[0]]


def pack_kernel(
    state_ref,
    faces_ref,
    pick_sub_ref,
    pick_curve_ref,
    compact_ref,
    sub_ref,
    lower_ref,
    upper_ref,
    pad,
):
    load_padded(state_ref, pad, 5)
    parts = [split(pad[c]) for c in range(5)]
    traces = [face_values(faces_ref[d], parts) for d in range(3)]
    picks = sent_faces(pick_sub_ref, pick_curve_ref)
    send_pack(traces, 5, picks, compact_ref[...], (sub_ref, lower_ref, upper_ref))


def node_places():
    numbers = lax.broadcasted_iota(jnp.int32, (128, ELEMENTS), 0)
    return (numbers % 5, (numbers // 5) % 5, numbers // 25)


def edge_signs():
    return [
        jnp.where(at == 4, 1.0 / EDGE, jnp.where(at == 0, -1.0 / EDGE, 0.0)) for at in node_places()
    ]


def deriv_sum(deriv_ref):
    high = [deriv_ref[d, :, 0:128] for d in range(3)]
    low = [deriv_ref[d, :, 128:256] for d in range(3)]
    none = jnp.zeros((128, 128), BF16)
    top = lanes([x for d in range(3) for x in (high[d], high[d])])
    return rows([top, lanes([x for d in range(3) for x in (low[d], none)])])


def dot_sum(a, parts):
    both = dot(a, rows(parts))
    return both[0:128] + both[128:256]


def volume_part(pad, deriv_ref, vol_ref, grad_ref, res):
    sign_ref = edge_signs()
    summed = deriv_sum(deriv_ref)
    none = jnp.zeros((128, 128), BF16)
    each = [
        rows(
            [
                lanes([deriv_ref[d, :, 0:128], deriv_ref[d, :, 0:128]]),
                lanes([deriv_ref[d, :, 128:256], none]),
            ]
        )
        for d in range(3)
    ]
    u = [pad[c] for c in range(5)]
    inverse, vel, pressure = point_values(u)
    total = u[4] + pressure
    enthalpy = total * inverse
    temperature = pressure * inverse
    fields = [u[0], vel[0], vel[1], vel[2], u[1], u[2], u[3], enthalpy, total, temperature]
    for f in range(0, 10, 2):
        pair = [split(fields[f]), split(fields[f + 1])]
        high, low = (lanes([pair[0][j], pair[1][j]]) for j in range(2))
        for d in range(3):
            res[d * 128 : (d + 1) * 128, f * 128 : (f + 2) * 128] = dot_two(each[d], high, low)

    def der(f, d):
        return res[d * 128 : (d + 1) * 128, f * 128 : (f + 1) * 128]

    for d in range(3):
        for v, f in enumerate((1, 2, 3, 9)):
            grad_ref[3 * v + d] = der(f, d) - sign_ref[d] * fields[f]
    div_vel = der(1, 0) + der(2, 1) + der(3, 2)
    div_mom = der(4, 0) + der(5, 1) + der(6, 2)
    advect = vel[0] * der(0, 0) + vel[1] * der(0, 1) + vel[2] * der(0, 2)
    carry = advect + div_mom
    mass = 0.5 * (u[0] * div_vel + carry)
    edge_mass = sign_ref[0] * u[1] + sign_ref[1] * u[2] + sign_ref[2] * u[3]
    vol_ref[0] = edge_mass - mass
    specific = [vel[0], vel[1], vel[2], enthalpy]
    full = [u[1], u[2], u[3], total]
    for k in range(4):
        cross = []
        direct = []
        edge = None
        for d in range(3):
            product = full[k] * vel[d]
            flux = product + pressure if k == d else product
            edge_d = sign_ref[d] * flux
            edge = edge_d if edge is None else edge + edge_d
            h, l = split(specific[k] * vel[d])
            cross += [h, l]
            h, l = split(product + 4.0 * pressure if k == d else product)
            direct += [h, l]
        both = dot_sum(summed, [lanes(list(p)) for p in zip(cross, direct)])
        f_spec, f_full = (1 + k, 4 + k) if k < 3 else (7, 8)
        quad = full[k] * div_vel + specific[k] * carry + u[0] * both[:, 0:128] + both[:, 128:256]
        for d in range(3):
            quad = quad + u[1 + d] * der(f_spec, d) + vel[d] * der(f_full, d)
        vol_ref[1 + k] = edge - 0.25 * quad


def partner_rows(index, d):
    peer = 256 + lax.shift_right_logical(index - 256, 2) * 16 + (index & 3) + 4 * d
    return jnp.where(index < 256, index, jnp.where(index < 288, peer, index + 96))


def gather_hot(partner_ref, kind_ref, hot, d):
    near = lax.broadcasted_iota(jnp.int32, (256, ELEMENTS), 0)
    far = near[0:192] + 256
    for q in range(4):
        for s in range(2):
            f = 2 * d + s
            row = partner_rows(partner_ref[f, q : q + 1, :], d)
            if q > 0:
                row = jnp.where(kind_ref[f : f + 1, :] == 2, row, -1)
            spot = slice(q * 256 + s * 128, q * 256 + (s + 1) * 128)
            hot[0:256, spot] = jnp.where(near == row, 1.0, 0.0).astype(BF16)
            hot[256:448, spot] = jnp.where(far == row, 1.0, 0.0).astype(BF16)


def remote_pool(sub_ref, lower_ref, upper_ref, spread, d):
    arrived = rows(
        [sub_ref[...], lower_ref[32 * d : 32 * d + 32, :], upper_ref[32 * d : 32 * d + 32, :]]
    )
    h, l = split(arrived)
    return dot_nt(spread, h).astype(BF16), dot_nt(spread, l).astype(BF16)


def surface_kernel(
    sub_ref,
    lower_ref,
    upper_ref,
    state_ref,
    deriv_ref,
    level_ref,
    kind_ref,
    partner_ref,
    quadrant_ref,
    faces_ref,
    spread_ref,
    quads_ref,
    project_ref,
    place_ref,
    pick_sub_ref,
    pick_curve_ref,
    compact_ref,
    acc_ref,
    flux_ref,
    sub_out,
    lower_out,
    upper_out,
    pad,
    res,
    hots,
    owns,
    gots,
    quads,
    grad,
):
    load_padded(state_ref, pad, 5)
    volume_part(pad, deriv_ref, acc_ref, grad, res)
    state_parts = [split(pad[c]) for c in range(5)]
    metric = 1.0 + level_ref[...].astype(F32)
    spare = jnp.where(
        lax.broadcasted_iota(jnp.int32, (32, ELEMENTS), 0) >= 25, 1.0, 0.0
    ).astype(F32)
    for d in range(3):
        own, got, quad, hot = (x.at[d] for x in (owns, gots, quads, hots))
        traces = face_values(faces_ref[d], state_parts)
        own[...] = traces[:, 0:640].astype(F32) + traces[:, 640:1280].astype(F32)
        near = pool_rows(traces, 5)
        gather_hot(partner_ref, kind_ref, hot, d)
        far = remote_pool(sub_ref, lower_ref, upper_ref, spread_ref[...], d)
        pool = rows([lanes([near[j], far[j]]) for j in range(2)])
        both = dot(pool, hot[...])
        got[...] = both[0:160] + both[160:320]
        big = lanes([kind_ref[2 * d + s : 2 * d + s + 1, :] for s in range(2)])
        big = jnp.broadcast_to(big, (32, 2 * ELEMENTS)) == 2
        parts = []
        for c in range(5):
            mine = lanes([own[s * 32 : s * 32 + 32, c * 128 : (c + 1) * 128] for s in range(2)])
            parts.append(split(jnp.where(big, mine, got[c * 32 : (c + 1) * 32, 0:256])))
        first_h = lanes([h for h, l in parts])
        first_l = lanes([l for h, l in parts])
        quad[...] = dot(quads_ref[...], rows([first_h, first_l, first_h]))
        stacks = {0: [], 1: []}
        for s in range(2):
            f = 2 * d + s
            sign = 2 * s - 1
            kind = jnp.broadcast_to(kind_ref[f : f + 1, :], (32, ELEMENTS))
            quarter = jnp.broadcast_to(quadrant_ref[f : f + 1, :], (32, ELEMENTS))
            is_big = kind == 2
            is_small = kind == 1
            for q in range(4):
                left, far = [], []
                for c in range(5):
                    spot = slice(c * 128, (c + 1) * 128)
                    wide = slice(c * 256 + s * 128, c * 256 + (s + 1) * 128)
                    minus = quad[32 * q : 32 * q + 32, wide]
                    plus = got[
                        c * 32 : (c + 1) * 32, q * 256 + s * 128 : q * 256 + (s + 1) * 128
                    ]
                    if q == 0:
                        minus = jnp.where(is_big, minus, own[s * 32 : s * 32 + 32, spot])
                        part = quad[96:128, wide]
                        for t in (2, 1, 0):
                            part = jnp.where(quarter == t, quad[32 * t : 32 * t + 32, wide], part)
                        plus = jnp.where(is_small, part, plus)
                    if c in (0, 4):
                        minus = minus + spare
                        plus = plus + spare
                    left.append(minus)
                    far.append(plus)
                if q > 0:
                    left[0] = jnp.where(is_big, left[0], 1.0)
                    far[0] = jnp.where(is_big, far[0], 1.0)
                inv_l, vel_l, press_l = point_values(left)
                inv_r, vel_r, press_r = point_values(far)
                temp_l, temp_r = press_l * inv_l, press_r * inv_r
                speed = jnp.maximum(
                    jnp.abs(vel_l[d]) + jnp.sqrt(1.4 * temp_l),
                    jnp.abs(vel_r[d]) + jnp.sqrt(1.4 * temp_r),
                )
                values = []
                for c in range(5):
                    if c == 0:
                        central = left[1 + d] + far[1 + d]
                    elif c == 4:
                        central = (left[4] + press_l) * vel_l[d] + (far[4] + press_r) * vel_r[d]
                    else:
                        central = left[c] * vel_l[d] + far[c] * vel_r[d]
                        if c == 1 + d:
                            central = central + (press_l + press_r)
                    jump = speed * (far[c] - left[c])
                    values.append(jump - central if sign > 0 else jump + central)
                for a, b in zip(vel_l + [temp_l], vel_r + [temp_r]):
                    values.append(a + b if sign > 0 else -a - b)
                picked = [split(jnp.where(is_big, v, 0.0)) for v in values]
                stacks[s, q] = [lanes([p[j] for p in picked]) for j in range(2)]
                if q == 0:
                    plain = lanes([jnp.where(is_big, 0.0, v) for v in values])
            stack_h = rows([stacks[s, q][0] for q in range(4)])
            stack_l = rows([stacks[s, q][1] for q in range(4)])
            value = plain + dot_two(project_ref[...], stack_h, stack_l)
            for j, part in enumerate(split(value)):
                stacks[j].append(part)
        lifted = dot(place_ref[d], rows(stacks[0] + stacks[1]))
        for c in range(5):
            acc_ref[c] = acc_ref[c] + lifted[:, c * 128 : (c + 1) * 128]
        for v in range(4):
            grad[3 * v + d] = metric * (
                grad[3 * v + d] + lifted[:, (5 + v) * 128 : (6 + v) * 128]
            )
    acc_ref.send()
    inverse = 1.0 / pad[0]
    vel = [pad[1 + k] * inverse for k in range(3)]
    divergence = (2.0 / 3.0 * viscosity) * (grad[0] + grad[4] + grad[8])
    for d in range(3):
        heat = conduction * grad[9 + d]
        for k in range(3):
            tau = viscosity * (grad[3 * d + k] + grad[3 * k + d])
            if k == d:
                tau = tau - divergence
            flux_ref[d, k] = tau
            heat = heat + vel[k] * tau
        flux_ref[d, 3] = heat
    flux_ref.send()
    traces = [
        face_values(faces_ref[d], [split(flux_ref[d, c]) for c in range(4)]) for d in range(3)
    ]
    picks = sent_faces(pick_sub_ref, pick_curve_ref)
    send_pack(traces, 4, picks, compact_ref[...], (sub_out, lower_out, upper_out))


def own_viscous_part(flux_ref, deriv_ref, acc):
    parts = []
    for d in range(3):
        plain = [split(flux_ref[d, c]) for c in range(4)]
        h = lanes([p[0] for p in plain])
        l = lanes([p[1] for p in plain])
        parts += [h, l]
    both = dot_sum(deriv_sum(deriv_ref), parts)
    half = [0.5 * sign for sign in edge_signs()]
    for c in range(4):
        value = both[:, c * 128 : (c + 1) * 128]
        for d in range(3):
            value = value - half[d] * flux_ref[d, c]
        acc[c] = value


def final_kernel(
    sub_ref,
    lower_ref,
    upper_ref,
    flux_ref,
    deriv_ref,
    faces_ref,
    kind_ref,
    partner_ref,
    spread_ref,
    quadrant_ref,
    mixers_ref,
    place_ref,
    level_ref,
    acc_in_ref,
    memory_ref,
    state_ref,
    state_out,
    memory_out,
    acc,
    hots,
):
    own_viscous_part(flux_ref, deriv_ref, acc)
    for d in range(3):
        hot = hots.at[d]
        traces = face_values(faces_ref[d], [split(flux_ref[d, c]) for c in range(4)])
        near = pool_rows(traces, 4)
        far = remote_pool(sub_ref, lower_ref, upper_ref, spread_ref[0:128, :], d)
        pool = [lanes([near[j], far[j]]) for j in range(2)]
        gather_hot(partner_ref, kind_ref, hot, d)
        got = dot(rows(pool), hot[...]).astype(BF16)
        ends = [[], []]
        for s in range(2):
            f = 2 * d + s
            kind = jnp.broadcast_to(kind_ref[f : f + 1, :], (32, ELEMENTS))
            quarter = jnp.broadcast_to(quadrant_ref[f : f + 1, :], (32, ELEMENTS))
            group = jnp.where(kind == 1, quarter + 1, jnp.where(kind == 2, 5, 0))
            wanted = [jnp.where(group == t, 1.0, 0.0).astype(BF16) for t in range(6)]
            stacks = []
            for j in range(2):
                blocks = []
                for b in range(9):
                    q = max(0, b - 5)
                    spot = slice(q * 256 + s * 128, q * 256 + (s + 1) * 128)
                    pieces = [
                        got[j * 128 + c * 32 : j * 128 + (c + 1) * 32, spot] for c in range(4)
                    ]
                    if b < 6:
                        pieces = [p * wanted[b] for p in pieces]
                    blocks.append(lanes(pieces))
                spot = slice(s * 128, (s + 1) * 128)
                blocks.append(
                    lanes([near[j][c * 32 : (c + 1) * 32, spot] * wanted[5] for c in range(4)])
                )
                stacks.append(rows(blocks))
            value = dot_two(mixers_ref[...], stacks[0], stacks[1])
            for j, part in enumerate(split(value)):
                ends[j].append(part)
        lifted = dot(place_ref[d], rows(ends[0] + ends[1]))
        for c in range(4):
            piece = lifted[:, c * 128 : (c + 1) * 128]
            acc[c] = acc[c] + piece
    metric = time_step * (1.0 + level_ref[...].astype(F32))
    for c in range(5):
        total = acc_in_ref[c] if c == 0 else acc_in_ref[c] + acc[c - 1]
        change = section_decay * memory_ref[c] + metric * total[0:125]
        memory_out[c] = change
        state_out[c] = state_ref[c] + section_weight * change


class Late:
    def __init__(self, near, copy):
        self.near, self.copy = near, copy

    def ready(self):
        if self.copy is not None:
            self.copy.wait()
            self.copy = None
        return self.near

    def __getitem__(self, key):
        return self.ready()[key]


class Early:
    def __init__(self, near, copy):
        self.near, self.copy = near, copy

    def send(self):
        self.copy.start()

    def __getitem__(self, key):
        return self.near[key]

    def __setitem__(self, key, value):
        self.near[key] = value


def placed(arrays):
    if INTERPRET:
        return arrays
    return [pltpu.with_memory_space_constraint(x, pltpu.VMEM) for x in arrays]


def call(body, outs, operands, scratch=(), arrived=(), early=0):
    counts = [len(arrived), len(operands), len(outs), len(operands), early, len(scratch)]

    def kernel(*refs):
        groups, at = [], 0
        for count in counts:
            groups.append(refs[at : at + count])
            at += count
        messages, far, out_refs, near, made, work = groups
        copies = [
            pltpu.make_async_copy(source, target, refs[at].at[i])
            for i, (source, target) in enumerate(zip(far, near))
        ]
        for copy in copies:
            copy.start()
        given = [Late(target, copy) for target, copy in zip(near, copies)]
        whole = [
            Early(source, pltpu.make_async_copy(source, target, refs[at].at[len(far) + i]))
            for i, (source, target) in enumerate(zip(made, out_refs))
        ]
        body(*messages, *given, *whole, *out_refs[early:], *work)
        for late in given:
            late.ready()
        for out in whole:
            out.copy.wait()

    return pl.pallas_call(
        kernel,
        out_shape=[jax.ShapeDtypeStruct(shape, F32) for shape in outs],
        in_specs=[pl.BlockSpec(memory_space=pltpu.VMEM)] * len(arrived)
        + [pl.BlockSpec(memory_space=pl.ANY)] * len(operands),
        out_specs=[pl.BlockSpec(memory_space=pl.ANY)] * early
        + [pl.BlockSpec(memory_space=pltpu.VMEM)] * (len(outs) - early),
        scratch_shapes=[pltpu.VMEM(x.shape, x.dtype) for x in operands]
        + [pltpu.VMEM(shape, F32) for shape in outs[:early]]
        + [pltpu.VMEM(*(o if isinstance(o[0], tuple) else (o, F32))) for o in scratch]
        + [pltpu.SemaphoreType.DMA((len(operands) + early,))],
        compiler_params=pltpu.CompilerParams(vmem_limit_bytes=VMEM_LIMIT),
        name=body.__name__,
        interpret=INTERPRET,
    )(*placed(arrived), *operands)


INTERPRET = False


def exchange(sub, lower, upper):
    count = lax.axis_size("curve")
    return (
        lax.all_to_all(sub, "sub", split_axis=0, concat_axis=0, tiled=True),
        lax.ppermute(lower, "curve", [(i, (i + 1) % count) for i in range(count)]),
        lax.ppermute(upper, "curve", [((i + 1) % count, i) for i in range(count)]),
    )


def local(
    state_now,
    section_memory,
    element_level,
    face_kind,
    face_partner,
    face_quadrant,
    send_sub,
    send_curve,
):
    const = {name: jnp.asarray(value) for name, value in constants().items()}
    level = element_level.reshape(1, ELEMENTS)
    picks = (send_sub.transpose(1, 2, 0), send_curve.transpose(1, 0, 2))
    face_partner = face_partner.transpose(1, 0, 2)
    messages = [(128, 128), (96, 128), (96, 128)]
    padded5 = (5, 128, ELEMENTS)
    hot = ((3, 448, 8 * ELEMENTS), BF16)
    sent = call(
        pack_kernel,
        messages,
        (state_now, const["faces"], *picks, const["compact_state"]),
        scratch=[padded5],
    )
    acc, flux, *sent = call(
        surface_kernel,
        [padded5, (3, 4, 128, ELEMENTS)] + messages,
        (
            state_now,
            const["deriv"],
            level,
            face_kind,
            face_partner,
            face_quadrant,
            const["faces"],
            const["spread"],
            const["quads"],
            const["project"],
            const["place_state"],
            *picks,
            const["compact_flux"],
        ),
        scratch=[
            padded5,
            (384, 1280),
            hot,
            (3, 64, 640),
            (3, 160, 1024),
            (3, 128, 1280),
            (12, 128, ELEMENTS),
        ],
        arrived=exchange(*sent),
        early=2,
    )
    state_next, memory_next = call(
        final_kernel,
        [(5, 125, ELEMENTS)] * 2,
        (
            flux,
            const["deriv"],
            const["faces"],
            face_kind,
            face_partner,
            const["spread"],
            face_quadrant,
            const["mixers"],
            const["place_flux"],
            level,
            acc,
            section_memory,
            state_now,
        ),
        scratch=[(4, 128, ELEMENTS), hot],
        arrived=exchange(*sent),
    )
    return (state_next, memory_next)


def solution(mesh):
    placed = (
        P(None, None, ("curve", "sub")),
        P(None, None, ("curve", "sub")),
        P(("curve", "sub")),
        P(None, ("curve", "sub")),
        P(None, None, ("curve", "sub")),
        P(None, ("curve", "sub")),
        P(("curve", "sub"), None, None),
        P(("curve", "sub"), None, None),
    )
    return jax.shard_map(
        local,
        mesh=mesh,
        in_specs=placed,
        out_specs=(P(None, None, ("curve", "sub")), P(None, None, ("curve", "sub"))),
        check_vma=False,
    )
```

```python
import functools
import math

import jax
import jax.numpy as jnp
import ml_dtypes
import numpy as np
from jax import lax
from jax.experimental import pallas as pl
from jax.experimental.pallas import tpu as pltpu
from jax.sharding import PartitionSpec as P

viscosity = 0.1
conduction = 0.1 * 1.4 / (0.4 * 0.72)
time_step = 0.02
section_decay = -567301805773.0 / 1357537059087.0
section_weight = 5161836677717.0 / 13612068292357.0
EDGE = 0.1
F32, BF16 = jnp.float32, jnp.bfloat16
ELEMENTS = 128
VMEM_LIMIT = 56 * 1024 * 1024


def node_tables():
    nodes = np.array([-1.0, -math.sqrt(3.0 / 7.0), 0.0, math.sqrt(3.0 / 7.0), 1.0])
    weights = np.array([0.1, 49.0 / 90.0, 32.0 / 45.0, 49.0 / 90.0, 0.1])
    prods = np.array(
        [np.prod([nodes[m] - nodes[k] for k in range(5) if k != m]) for m in range(5)]
    )
    deriv = np.zeros((5, 5))
    for i in range(5):
        for m in range(5):
            if i != m:
                deriv[i, m] = prods[i] / prods[m] / (nodes[i] - nodes[m])
        deriv[i, i] = -np.sum(deriv[i])

    def lagrange(points):
        values = np.ones((5, 5))
        for m in range(5):
            for k in range(5):
                if k != m:
                    values[:, m] = values[:, m] * (points - nodes[k]) / (nodes[m] - nodes[k])
        return values

    halves = [lagrange((nodes - 1.0) / 2.0), lagrange((nodes + 1.0) / 2.0)]
    projs = [0.5 * (h * weights[:, None]).T / weights[:, None] for h in halves]
    interp = [np.kron(halves[a], halves[b]) for a in range(2) for b in range(2)]
    project = [np.kron(projs[a], projs[b]) for a in range(2) for b in range(2)]
    return deriv, interp, project


def padded(matrix, rows, cols):
    out = np.zeros((rows, cols))
    out[: matrix.shape[0], : matrix.shape[1]] = matrix
    return out


def split_np(matrix):
    high = matrix.astype(np.float32).astype(ml_dtypes.bfloat16)
    low = (matrix - high.astype(np.float64)).astype(np.float32).astype(ml_dtypes.bfloat16)
    return high, low


def stack3(matrix):
    high, low = split_np(matrix)
    return np.concatenate([high, high, low], axis=1)


def stack2(matrix):
    high, low = split_np(matrix)
    top = np.concatenate([high, high], axis=1)
    return np.concatenate([top, np.concatenate([low, np.zeros_like(low)], axis=1)], axis=0)


@functools.lru_cache(maxsize=None)
def constants():
    deriv, interp, project = node_tables()
    eye5 = np.eye(5)
    big = [
        np.kron(np.kron(eye5, eye5), deriv),
        np.kron(np.kron(eye5, deriv), eye5),
        np.kron(np.kron(deriv, eye5), eye5),
    ]
    index = np.arange(125)
    coord = [index % 5, (index // 5) % 5, index // 25]
    trace = {}
    for d in range(3):
        for s in range(2):
            rows = index[coord[d] == 4 * s]
            t = np.zeros((25, 125))
            t[np.arange(25), rows] = 1.0
            trace[d, s] = t
    sigma = (-1.0, 1.0)
    out = {}
    out["deriv"] = np.stack(
        [np.concatenate(split_np(padded(big[d], 128, 128)), axis=1) for d in range(3)]
    )
    spread = np.zeros((160, 128))
    for c in range(5):
        spread[c * 32 : c * 32 + 25, c * 25 : c * 25 + 25] = np.eye(25)
    out["spread"] = spread.astype(ml_dtypes.bfloat16)
    for comps, name in ((5, "compact_state"), (4, "compact_flux")):
        out[name] = np.tile(spread[: 32 * comps].T, (1, 2)).astype(ml_dtypes.bfloat16)
    out["quads"] = stack3(np.concatenate([padded(interp[q], 32, 32) for q in range(4)], axis=0))
    out["project"] = stack2(np.concatenate([padded(project[q], 32, 32) for q in range(4)], axis=1))
    both = sum(project[q] @ interp[q] for q in range(4))
    mixers = [np.eye(25)] + interp + project + [both - np.eye(25)]
    out["mixers"] = stack2(np.concatenate([padded(m, 32, 32) for m in mixers], axis=1))
    out["faces"] = np.stack(
        [
            np.concatenate([padded(trace[d, s], 32, 128) for s in range(2)], axis=0)
            for d in range(3)
        ]
    ).astype(ml_dtypes.bfloat16)
    for name, signed in (("place_state", False), ("place_flux", True)):
        out[name] = np.stack(
            [
                np.concatenate(
                    [
                        padded((sigma[s] if signed else 1.0) * 5.0 * trace[d, s].T, 128, 32)
                        for s in (0, 1, 0, 1)
                    ],
                    axis=1,
                )
                for d in range(3)
            ]
        ).astype(ml_dtypes.bfloat16)
    return out


def split(x):
    high = x.astype(BF16)
    return high, (x - high.astype(F32)).astype(BF16)


def dot(a, b):
    return lax.dot_general(a, b, (((1,), (0,)), ((), ())), preferred_element_type=F32)


def dot_two(a, high, low):
    both = dot(a, rows([high, low]))
    half = a.shape[0] // 2
    return both[0:half] + both[half:]


def dot_nt(a, b):
    return lax.dot_general(a, b, (((1,), (1,)), ((), ())), preferred_element_type=F32)


def lanes(parts):
    return jnp.concatenate(parts, axis=1)


def rows(parts):
    return jnp.concatenate(parts, axis=0)


def one_hot(index_row, count):
    width = index_row.shape[1]
    numbers = lax.broadcasted_iota(jnp.int32, (count, width), 0)
    return jnp.where(numbers == index_row, 1.0, 0.0).astype(BF16)


def load_padded(ref, pad, count):
    for c in range(count):
        pad[c, 120:128, :] = jnp.full((8, ELEMENTS), 1.0 if c in (0, 4) else 0.0, F32)
        pad[c, 0:125, :] = ref[c]


def point_values(u):
    inverse = 1.0 / u[0]
    vel = [u[1 + k] * inverse for k in range(3)]
    kinetic = u[1] * vel[0] + u[2] * vel[1] + u[3] * vel[2]
    pressure = 0.4 * (u[4] - 0.5 * kinetic)
    return inverse, vel, pressure


def sent_faces(sub_ref, curve_ref):
    place = lax.broadcasted_iota(jnp.int32, (1, 128), 1)
    spot = lax.broadcasted_iota(jnp.int32, (4, 128), 0)
    peer = lax.broadcasted_iota(jnp.int32, (8, 128), 1)
    peers = jnp.where(
        lax.shift_right_logical(peer, 4) == lax.broadcasted_iota(jnp.int32, (8, 128), 0), 1.0, 0.0
    ).astype(BF16)
    slot = lax.broadcasted_iota(jnp.int32, (32, 128), 1)
    slots = jnp.where(
        (slot & 31) == lax.broadcasted_iota(jnp.int32, (32, 128), 0), 1.0, 0.0
    ).astype(BF16)
    sub, lower, upper = [], [], []
    for d in range(3):
        wide = dot(sub_ref[d].astype(F32).astype(BF16), peers)
        wide = jnp.where((place & 3) == spot, wide, 0.0)
        row = jnp.sum(wide, axis=0, keepdims=True).astype(jnp.int32)
        sub.append(jnp.where((lax.shift_right_logical(place, 2) & 3) == d, row, -1))
        wide = dot(curve_ref[d].astype(F32).astype(BF16), slots).astype(jnp.int32)
        here = lax.shift_right_logical(place, 5) == d
        lower.append(jnp.where(here, wide[1:2], -1))
        upper.append(jnp.where(here, wide[0:1], -1))
    return sub, lower, upper


def face_values(faces, parts):
    return dot(faces, lanes([p[0] for p in parts] + [p[1] for p in parts])).astype(BF16)


def pool_rows(traces, count):
    def block(j, c):
        spot = slice((j * count + c) * 128, (j * count + c + 1) * 128)
        return lanes([traces[0:32, spot], traces[32:64, spot]])

    return [rows([block(j, c) for c in range(count)]) for j in range(2)]


def send_hot(sub_ref, curve_ref):
    picks = sent_faces(sub_ref, curve_ref)
    return lanes([rows([one_hot(picks[t][d], 256) for d in range(3)]) for t in range(3)])


def send_pack(traces, count, hot, compact, outs):
    data = lanes([rows(pool_rows(traces[d], count)) for d in range(3)])
    found = dot(compact, dot(data, hot).astype(BF16))
    for t in range(3):
        outs[t][...] = jnp.transpose(found[:, t * 128 : (t + 1) * 128])[0 : outs[t].shape[0]]


def pack_kernel(
    pick_sub_ref,
    pick_curve_ref,
    state_ref,
    faces_ref,
    compact_ref,
    sub_ref,
    lower_ref,
    upper_ref,
    pad,
):
    hot = send_hot(pick_sub_ref, pick_curve_ref)
    load_padded(state_ref, pad, 5)
    parts = [split(pad[c]) for c in range(5)]
    traces = [face_values(faces_ref[d], parts) for d in range(3)]
    send_pack(traces, 5, hot, compact_ref[...], (sub_ref, lower_ref, upper_ref))


def node_places():
    numbers = lax.broadcasted_iota(jnp.int32, (128, ELEMENTS), 0)
    return (numbers % 5, (numbers // 5) % 5, numbers // 25)


def edge_signs():
    return [
        jnp.where(at == 4, 1.0 / EDGE, jnp.where(at == 0, -1.0 / EDGE, 0.0)) for at in node_places()
    ]


def deriv_sum(deriv_ref):
    high = [deriv_ref[d, :, 0:128] for d in range(3)]
    low = [deriv_ref[d, :, 128:256] for d in range(3)]
    none = jnp.zeros((128, 128), BF16)
    top = lanes([x for d in range(3) for x in (high[d], high[d])])
    return rows([top, lanes([x for d in range(3) for x in (low[d], none)])])


def dot_sum(a, parts):
    both = dot(a, rows(parts))
    return both[0:128] + both[128:256]


def volume_part(pad, deriv_ref, vol_ref, grad_ref, res):
    sign_ref = edge_signs()
    summed = deriv_sum(deriv_ref)
    none = jnp.zeros((128, 128), BF16)
    each = [
        rows(
            [
                lanes([deriv_ref[d, :, 0:128], deriv_ref[d, :, 0:128]]),
                lanes([deriv_ref[d, :, 128:256], none]),
            ]
        )
        for d in range(3)
    ]
    u = [pad[c] for c in range(5)]
    inverse, vel, pressure = point_values(u)
    total = u[4] + pressure
    enthalpy = total * inverse
    temperature = pressure * inverse
    fields = [u[0], vel[0], vel[1], vel[2], u[1], u[2], u[3], enthalpy, total, temperature]
    for f in range(0, 10, 2):
        pair = [split(fields[f]), split(fields[f + 1])]
        high, low = (lanes([pair[0][j], pair[1][j]]) for j in range(2))
        for d in range(3):
            res[d * 128 : (d + 1) * 128, f * 128 : (f + 2) * 128] = dot_two(each[d], high, low)

    def der(f, d):
        return res[d * 128 : (d + 1) * 128, f * 128 : (f + 1) * 128]

    for d in range(3):
        for v, f in enumerate((1, 2, 3, 9)):
            grad_ref[3 * v + d] = der(f, d) - sign_ref[d] * fields[f]
            grad_ref.send(3 * v + d)
    div_vel = der(1, 0) + der(2, 1) + der(3, 2)
    div_mom = der(4, 0) + der(5, 1) + der(6, 2)
    advect = vel[0] * der(0, 0) + vel[1] * der(0, 1) + vel[2] * der(0, 2)
    carry = advect + div_mom
    mass = 0.5 * (u[0] * div_vel + carry)
    edge_mass = sign_ref[0] * u[1] + sign_ref[1] * u[2] + sign_ref[2] * u[3]
    vol_ref[0] = edge_mass - mass
    vol_ref.send(0)
    specific = [vel[0], vel[1], vel[2], enthalpy]
    full = [u[1], u[2], u[3], total]
    for k in range(4):
        cross = []
        direct = []
        edge = None
        for d in range(3):
            product = full[k] * vel[d]
            flux = product + pressure if k == d else product
            edge_d = sign_ref[d] * flux
            edge = edge_d if edge is None else edge + edge_d
            h, l = split(specific[k] * vel[d])
            cross += [h, l]
            h, l = split(product + 4.0 * pressure if k == d else product)
            direct += [h, l]
        both = dot_sum(summed, [lanes(list(p)) for p in zip(cross, direct)])
        f_spec, f_full = (1 + k, 4 + k) if k < 3 else (7, 8)
        quad = full[k] * div_vel + specific[k] * carry + u[0] * both[:, 0:128] + both[:, 128:256]
        for d in range(3):
            quad = quad + u[1 + d] * der(f_spec, d) + vel[d] * der(f_full, d)
        vol_ref[1 + k] = edge - 0.25 * quad
        vol_ref.send(1 + k)


def volume_kernel(state_ref, deriv_ref, vol_ref, grad_ref, pad, res):
    load_padded(state_ref, pad, 5)
    volume_part(pad, deriv_ref, vol_ref, grad_ref, res)


def partner_rows(index, d):
    peer = 256 + lax.shift_right_logical(index - 256, 2) * 16 + (index & 3) + 4 * d
    return jnp.where(index < 256, index, jnp.where(index < 288, peer, index + 96))


def gather_hot(partner_ref, kind_ref, hot, d):
    near = lax.broadcasted_iota(jnp.int32, (256, ELEMENTS), 0)
    far = near[0:192] + 256
    for q in range(4):
        for s in range(2):
            f = 2 * d + s
            row = partner_rows(partner_ref[f, q : q + 1, :], d)
            if q > 0:
                row = jnp.where(kind_ref[f : f + 1, :] == 2, row, -1)
            spot = slice(q * 256 + s * 128, q * 256 + (s + 1) * 128)
            hot[0:256, spot] = jnp.where(near == row, 1.0, 0.0).astype(BF16)
            hot[256:448, spot] = jnp.where(far == row, 1.0, 0.0).astype(BF16)


def remote_pool(sub_ref, lower_ref, upper_ref, spread, d):
    arrived = rows(
        [sub_ref[...], lower_ref[32 * d : 32 * d + 32, :], upper_ref[32 * d : 32 * d + 32, :]]
    )
    h, l = split(arrived)
    return dot_nt(spread, h).astype(BF16), dot_nt(spread, l).astype(BF16)


def surface_kernel(
    sub_ref,
    lower_ref,
    upper_ref,
    kind_ref,
    partner_ref,
    state_ref,
    faces_ref,
    spread_ref,
    quads_ref,
    quadrant_ref,
    project_ref,
    place_ref,
    level_ref,
    vol_ref,
    grad_in_ref,
    pick_sub_ref,
    pick_curve_ref,
    compact_ref,
    acc_ref,
    flux_ref,
    sub_out,
    lower_out,
    upper_out,
    pad,
    hots,
    owns,
    gots,
    quads,
    grad,
):
    for d in range(3):
        gather_hot(partner_ref, kind_ref, hots.at[d], d)
    load_padded(state_ref, pad, 5)
    state_parts = [split(pad[c]) for c in range(5)]
    metric = 1.0 + level_ref[...].astype(F32)
    spare = jnp.where(
        lax.broadcasted_iota(jnp.int32, (32, ELEMENTS), 0) >= 25, 1.0, 0.0
    ).astype(F32)
    for d in range(3):
        own, got, quad, hot = (x.at[d] for x in (owns, gots, quads, hots))
        traces = face_values(faces_ref[d], state_parts)
        own[...] = traces[:, 0:640].astype(F32) + traces[:, 640:1280].astype(F32)
        near = pool_rows(traces, 5)
        far = remote_pool(sub_ref, lower_ref, upper_ref, spread_ref[...], d)
        pool = rows([lanes([near[j], far[j]]) for j in range(2)])
        both = dot(pool, hot[...])
        got[...] = both[0:160] + both[160:320]
        big = lanes([kind_ref[2 * d + s : 2 * d + s + 1, :] for s in range(2)])
        big = jnp.broadcast_to(big, (32, 2 * ELEMENTS)) == 2
        parts = []
        for c in range(5):
            mine = lanes([own[s * 32 : s * 32 + 32, c * 128 : (c + 1) * 128] for s in range(2)])
            parts.append(split(jnp.where(big, mine, got[c * 32 : (c + 1) * 32, 0:256])))
        first_h = lanes([h for h, l in parts])
        first_l = lanes([l for h, l in parts])
        quad[...] = dot(quads_ref[...], rows([first_h, first_l, first_h]))
        stacks = {0: [], 1: []}
        for s in range(2):
            f = 2 * d + s
            sign = 2 * s - 1
            kind = jnp.broadcast_to(kind_ref[f : f + 1, :], (32, ELEMENTS))
            quarter = jnp.broadcast_to(quadrant_ref[f : f + 1, :], (32, ELEMENTS))
            is_big = kind == 2
            is_small = kind == 1
            for q in range(4):
                left, far = [], []
                for c in range(5):
                    spot = slice(c * 128, (c + 1) * 128)
                    wide = slice(c * 256 + s * 128, c * 256 + (s + 1) * 128)
                    minus = quad[32 * q : 32 * q + 32, wide]
                    plus = got[
                        c * 32 : (c + 1) * 32, q * 256 + s * 128 : q * 256 + (s + 1) * 128
                    ]
                    if q == 0:
                        minus = jnp.where(is_big, minus, own[s * 32 : s * 32 + 32, spot])
                        part = quad[96:128, wide]
                        for t in (2, 1, 0):
                            part = jnp.where(quarter == t, quad[32 * t : 32 * t + 32, wide], part)
                        plus = jnp.where(is_small, part, plus)
                    if c in (0, 4):
                        minus = minus + spare
                        plus = plus + spare
                    left.append(minus)
                    far.append(plus)
                if q > 0:
                    left[0] = jnp.where(is_big, left[0], 1.0)
                    far[0] = jnp.where(is_big, far[0], 1.0)
                inv_l, vel_l, press_l = point_values(left)
                inv_r, vel_r, press_r = point_values(far)
                temp_l, temp_r = press_l * inv_l, press_r * inv_r
                speed = jnp.maximum(
                    jnp.abs(vel_l[d]) + jnp.sqrt(1.4 * temp_l),
                    jnp.abs(vel_r[d]) + jnp.sqrt(1.4 * temp_r),
                )
                values = []
                for c in range(5):
                    if c == 0:
                        central = left[1 + d] + far[1 + d]
                    elif c == 4:
                        central = (left[4] + press_l) * vel_l[d] + (far[4] + press_r) * vel_r[d]
                    else:
                        central = left[c] * vel_l[d] + far[c] * vel_r[d]
                        if c == 1 + d:
                            central = central + (press_l + press_r)
                    jump = speed * (far[c] - left[c])
                    values.append(jump - central if sign > 0 else jump + central)
                for a, b in zip(vel_l + [temp_l], vel_r + [temp_r]):
                    values.append(a + b if sign > 0 else -a - b)
                picked = [split(jnp.where(is_big, v, 0.0)) for v in values]
                stacks[s, q] = [lanes([p[j] for p in picked]) for j in range(2)]
                if q == 0:
                    plain = lanes([jnp.where(is_big, 0.0, v) for v in values])
            stack_h = rows([stacks[s, q][0] for q in range(4)])
            stack_l = rows([stacks[s, q][1] for q in range(4)])
            value = plain + dot_two(project_ref[...], stack_h, stack_l)
            for j, part in enumerate(split(value)):
                stacks[j].append(part)
        lifted = dot(place_ref[d], rows(stacks[0] + stacks[1]))
        for c in range(5):
            before = vol_ref[c] if d == 0 else acc_ref[c]
            acc_ref[c] = before + lifted[:, c * 128 : (c + 1) * 128]
            if d == 2:
                acc_ref.send(c)
        for v in range(4):
            grad[3 * v + d] = metric * (
                grad_in_ref[3 * v + d] + lifted[:, (5 + v) * 128 : (6 + v) * 128]
            )
    inverse = 1.0 / pad[0]
    vel = [pad[1 + k] * inverse for k in range(3)]
    divergence = (2.0 / 3.0 * viscosity) * (grad[0] + grad[4] + grad[8])
    for d in range(3):
        heat = conduction * grad[9 + d]
        for k in range(3):
            tau = viscosity * (grad[3 * d + k] + grad[3 * k + d])
            if k == d:
                tau = tau - divergence
            flux_ref[d, k] = tau
            heat = heat + vel[k] * tau
        flux_ref[d, 3] = heat
        flux_ref.send(d)
    traces = [
        face_values(faces_ref[d], [split(flux_ref[d, c]) for c in range(4)]) for d in range(3)
    ]
    hot = send_hot(pick_sub_ref, pick_curve_ref)
    send_pack(traces, 4, hot, compact_ref[...], (sub_out, lower_out, upper_out))


def own_viscous_part(flux_ref, deriv_ref, acc):
    parts = []
    for d in range(3):
        plain = [split(flux_ref[d, c]) for c in range(4)]
        h = lanes([p[0] for p in plain])
        l = lanes([p[1] for p in plain])
        parts += [h, l]
    both = dot_sum(deriv_sum(deriv_ref), parts)
    half = [0.5 * sign for sign in edge_signs()]
    for c in range(4):
        value = both[:, c * 128 : (c + 1) * 128]
        for d in range(3):
            value = value - half[d] * flux_ref[d, c]
        acc[c] = value


def final_kernel(
    sub_ref,
    lower_ref,
    upper_ref,
    kind_ref,
    partner_ref,
    flux_ref,
    deriv_ref,
    faces_ref,
    spread_ref,
    quadrant_ref,
    mixers_ref,
    place_ref,
    level_ref,
    acc_in_ref,
    memory_ref,
    state_ref,
    state_out,
    memory_out,
    acc,
    hots,
):
    for d in range(3):
        gather_hot(partner_ref, kind_ref, hots.at[d], d)
    own_viscous_part(flux_ref, deriv_ref, acc)
    for d in range(3):
        hot = hots.at[d]
        traces = face_values(faces_ref[d], [split(flux_ref[d, c]) for c in range(4)])
        near = pool_rows(traces, 4)
        far = remote_pool(sub_ref, lower_ref, upper_ref, spread_ref[0:128, :], d)
        pool = [lanes([near[j], far[j]]) for j in range(2)]
        got = dot(rows(pool), hot[...]).astype(BF16)
        ends = [[], []]
        for s in range(2):
            f = 2 * d + s
            kind = jnp.broadcast_to(kind_ref[f : f + 1, :], (32, ELEMENTS))
            quarter = jnp.broadcast_to(quadrant_ref[f : f + 1, :], (32, ELEMENTS))
            group = jnp.where(kind == 1, quarter + 1, jnp.where(kind == 2, 5, 0))
            wanted = [jnp.where(group == t, 1.0, 0.0).astype(BF16) for t in range(6)]
            stacks = []
            for j in range(2):
                blocks = []
                for b in range(9):
                    q = max(0, b - 5)
                    spot = slice(q * 256 + s * 128, q * 256 + (s + 1) * 128)
                    pieces = [
                        got[j * 128 + c * 32 : j * 128 + (c + 1) * 32, spot] for c in range(4)
                    ]
                    if b < 6:
                        pieces = [p * wanted[b] for p in pieces]
                    blocks.append(lanes(pieces))
                spot = slice(s * 128, (s + 1) * 128)
                blocks.append(
                    lanes([near[j][c * 32 : (c + 1) * 32, spot] * wanted[5] for c in range(4)])
                )
                stacks.append(rows(blocks))
            value = dot_two(mixers_ref[...], stacks[0], stacks[1])
            for j, part in enumerate(split(value)):
                ends[j].append(part)
        lifted = dot(place_ref[d], rows(ends[0] + ends[1]))
        for c in range(4):
            piece = lifted[:, c * 128 : (c + 1) * 128]
            acc[c] = acc[c] + piece
    metric = time_step * (1.0 + level_ref[...].astype(F32))
    for c in range(5):
        total = acc_in_ref[c] if c == 0 else acc_in_ref[c] + acc[c - 1]
        change = section_decay * memory_ref[c] + metric * total[0:125]
        memory_out[c] = change
        memory_out.send(c)
        state_out[c] = state_ref[c] + section_weight * change
        state_out.send(c)


class Late:
    def __init__(self, near, copy):
        self.near, self.copy = near, copy

    def ready(self):
        if self.copy is not None:
            self.copy.wait()
            self.copy = None
        return self.near

    def __getitem__(self, key):
        return self.ready()[key]


class Early:
    def __init__(self, near, copies):
        self.near, self.copies = near, copies

    def send(self, i):
        self.copies[i].start()

    def __getitem__(self, key):
        return self.near[key]

    def __setitem__(self, key, value):
        self.near[key] = value


def placed(arrays):
    if INTERPRET:
        return arrays
    return [pltpu.with_memory_space_constraint(x, pltpu.VMEM) for x in arrays]


def call(body, outs, operands, scratch=(), arrived=(), early=0):
    counts = [len(arrived), len(operands), len(outs), len(operands), early, len(scratch)]

    def kernel(*refs):
        groups, at = [], 0
        for count in counts:
            groups.append(refs[at : at + count])
            at += count
        messages, far, out_refs, near, made, work = groups
        copies = [
            pltpu.make_async_copy(source, target, refs[at].at[i])
            for i, (source, target) in enumerate(zip(far, near))
        ]
        for copy in copies:
            copy.start()
        given = [Late(target, copy) for target, copy in zip(near, copies)]
        whole, used = [], len(far)
        for source, target in zip(made, out_refs):
            count = source.shape[0]
            whole.append(
                Early(
                    source,
                    [
                        pltpu.make_async_copy(source.at[i], target.at[i], refs[at].at[used + i])
                        for i in range(count)
                    ],
                )
            )
            used += count
        body(*messages, *given, *whole, *out_refs[early:], *work)
        for late in given:
            late.ready()
        for out in whole:
            for copy in out.copies:
                copy.wait()

    return pl.pallas_call(
        kernel,
        out_shape=[jax.ShapeDtypeStruct(shape, F32) for shape in outs],
        in_specs=[pl.BlockSpec(memory_space=pltpu.VMEM)] * len(arrived)
        + [pl.BlockSpec(memory_space=pl.ANY)] * len(operands),
        out_specs=[pl.BlockSpec(memory_space=pl.ANY)] * early
        + [pl.BlockSpec(memory_space=pltpu.VMEM)] * (len(outs) - early),
        scratch_shapes=[pltpu.VMEM(x.shape, x.dtype) for x in operands]
        + [pltpu.VMEM(shape, F32) for shape in outs[:early]]
        + [pltpu.VMEM(*(o if isinstance(o[0], tuple) else (o, F32))) for o in scratch]
        + [pltpu.SemaphoreType.DMA((len(operands) + sum(shape[0] for shape in outs[:early]),))],
        compiler_params=pltpu.CompilerParams(vmem_limit_bytes=VMEM_LIMIT),
        name=body.__name__,
        interpret=INTERPRET,
    )(*placed(arrived), *operands)


INTERPRET = False


def exchange(sub, lower, upper):
    count = lax.axis_size("curve")
    return (
        lax.all_to_all(sub, "sub", split_axis=0, concat_axis=0, tiled=True),
        lax.ppermute(lower, "curve", [(i, (i + 1) % count) for i in range(count)]),
        lax.ppermute(upper, "curve", [((i + 1) % count, i) for i in range(count)]),
    )


def local(
    state_now,
    section_memory,
    element_level,
    face_kind,
    face_partner,
    face_quadrant,
    send_sub,
    send_curve,
):
    const = {name: jnp.asarray(value) for name, value in constants().items()}
    level = element_level.reshape(1, ELEMENTS)
    picks = (send_sub.transpose(1, 2, 0), send_curve.transpose(1, 0, 2))
    face_partner = face_partner.transpose(1, 0, 2)
    messages = [(128, 128), (96, 128), (96, 128)]
    padded5 = (5, 128, ELEMENTS)
    hot = ((3, 448, 8 * ELEMENTS), BF16)
    sent = call(
        pack_kernel,
        messages,
        (*picks, state_now, const["faces"], const["compact_state"]),
        scratch=[padded5],
    )
    arrived = exchange(*sent)
    volume, gradients = call(
        volume_kernel,
        [padded5, (12, 128, ELEMENTS)],
        (state_now, const["deriv"]),
        scratch=[padded5, (384, 1280)],
        early=2,
    )
    acc, flux, *sent = call(
        surface_kernel,
        [padded5, (3, 4, 128, ELEMENTS)] + messages,
        (
            face_kind,
            face_partner,
            state_now,
            const["faces"],
            const["spread"],
            const["quads"],
            face_quadrant,
            const["project"],
            const["place_state"],
            level,
            volume,
            gradients,
            *picks,
            const["compact_flux"],
        ),
        scratch=[
            padded5,
            hot,
            (3, 64, 640),
            (3, 160, 1024),
            (3, 128, 1280),
            (12, 128, ELEMENTS),
        ],
        arrived=arrived,
        early=2,
    )
    state_next, memory_next = call(
        final_kernel,
        [(5, 125, ELEMENTS)] * 2,
        (
            face_kind,
            face_partner,
            flux,
            const["deriv"],
            const["faces"],
            const["spread"],
            face_quadrant,
            const["mixers"],
            const["place_flux"],
            level,
            acc,
            section_memory,
            state_now,
        ),
        scratch=[(4, 128, ELEMENTS), hot],
        arrived=exchange(*sent),
        early=2,
    )
    return (state_next, memory_next)


def solution(mesh):
    placed = (
        P(None, None, ("curve", "sub")),
        P(None, None, ("curve", "sub")),
        P(("curve", "sub")),
        P(None, ("curve", "sub")),
        P(None, None, ("curve", "sub")),
        P(None, ("curve", "sub")),
        P(("curve", "sub"), None, None),
        P(("curve", "sub"), None, None),
    )
    return jax.shard_map(
        local,
        mesh=mesh,
        in_specs=placed,
        out_specs=(P(None, None, ("curve", "sub")), P(None, None, ("curve", "sub"))),
        check_vma=False,
    )
```
